512 devices in a mesh: fsdp: 128 (over z, y, core), rep: 4 (over x).
Axes of the slice: x: 4, y: 4, z: 16, core: 2. Of those that a mesh axis runs over, the one named last changes fastest.
Arguments:
- grad: float32 [128, 512, 512], P(None, 'fsdp'), may hold values from -6 to 6
- left_factor: float32 [256, 512, 512], P('fsdp', 'rep')
- right_factor: float32 [256, 512, 512], P('fsdp', 'rep')
- left_root: float32 [256, 512, 512], P('fsdp', 'rep'), as said below
- right_root: float32 [256, 512, 512], P('fsdp', 'rep'), as said below
- owner_table: int32 [128], replicated, may hold values from 0 to 127, as said below
Outputs:
- new_left: float32 [256, 512, 512], P('fsdp', 'rep')
- new_right: float32 [256, 512, 512], P('fsdp', 'rep')
- direction: float32 [128, 512, 512], P(None, 'fsdp', 'rep')
The draws below stay inside these ranges and needn't reach their ends.
Inputs may be any that keep to these rules, and one draw needn't show every extreme that they name: `owner_table`: each fsdp index owns at most 2 blocks, and some index owns exactly 2. Every matrix right_root[i] is symmetric. Every matrix left_root[i] is symmetric.
All inputs are finite; a program needn't handle non-finite values.
Results may differ from the reference program's by a relative error of at most 0.00007.
Values sent between devices are 32-bit elements; how exact they have to be, the bound alone decides.
A program may use at most 64 MiB of HBM per device.

```python
import jax
import jax.numpy as jnp
from jax import lax

BLK = 512
MOST = 2
NB = 128
HOMES = 256


def symmetric_blocks(key, lowest, highest, spread):
    key_diag, key_rest = jax.random.split(key)
    diagonal = jax.random.uniform(key_diag, (HOMES, BLK), jnp.float32, lowest, highest)
    rough = jax.random.uniform(key_rest, (HOMES, BLK, BLK), jnp.float32, -spread, spread)
    mirrored = (rough + jnp.swapaxes(rough, 1, 2)) * 0.5
    on_diag = jnp.arange(BLK)[:, None] == jnp.arange(BLK)[None, :]
    return jnp.where(on_diag[None, :, :], diagonal[:, :, None], mirrored)


def draw_left_factor(key, part):
    key = jax.random.fold_in(key, 3)
    return symmetric_blocks(key, 0.5, 1.5, 1.0 / BLK)


def draw_right_factor(key, part):
    key = jax.random.fold_in(key, 5)
    return symmetric_blocks(key, 0.5, 1.5, 1.0 / BLK)


def draw_left_root(key, part):
    key = jax.random.fold_in(key, 7)
    return symmetric_blocks(key, 1.0, 2.0, 1.0 / BLK)


def draw_right_root(key, part):
    key = jax.random.fold_in(key, 9)
    return symmetric_blocks(key, 1.0, 2.0, 1.0 / BLK)


def draw_owner_table(key, part):
    key = jax.random.fold_in(key, 11)
    key_pairs, key_owners, key_order = jax.random.split(key, 3)
    pairs = jax.random.randint(key_pairs, (), max(1, NB // 8), NB // 4 + 1)
    owners = jax.random.permutation(key_owners, jnp.arange(NB, dtype=jnp.int32))
    numbers = jnp.arange(NB, dtype=jnp.int32)
    picked = jnp.where(numbers < 2 * pairs, numbers // 2, numbers - pairs)
    sequence = owners[picked]
    shuffle = jax.random.permutation(key_order, jnp.arange(NB, dtype=jnp.int32))
    return jnp.zeros((NB,), jnp.int32).at[shuffle].set(sequence)


def block_scale(key, extent, cuts, smallest, top_value):
    gain, own = 1.0, jax.random.fold_in(key, 6)
    for axis_at, blocks in cuts:
        steps = jnp.exp(jax.random.uniform(jax.random.fold_in(own, axis_at), (blocks,), jnp.float32, smallest / len(cuts), top_value / len(cuts)))
        gain = gain * jnp.repeat(steps, extent[axis_at] // blocks).reshape([-1 if axis == axis_at else 1 for axis in range(len(extent))])
    return gain


def gaussian(key, dims, scale, most, shards=(), held_as=jnp.bfloat16):
    factor_of = block_scale(key, dims, shards, -0.22, 0.18) if shards else 1.0
    values = jax.random.normal(key, dims, jnp.float32) * scale * factor_of
    return jnp.minimum(jnp.maximum(values, -most), most).astype(held_as)


def setup_inputs(seed: int = 0) -> dict:
    seeds = jax.random.split(jax.random.key(seed), 7)
    grad = gaussian(seeds[0], (NB, BLK, BLK), 1.0, 6.0, ((1, 128),), jnp.float32)
    left_factor = draw_left_factor(jax.random.fold_in(seeds[6], 71), 0)
    right_factor = draw_right_factor(jax.random.fold_in(seeds[6], 71), 0)
    left_root = draw_left_root(jax.random.fold_in(seeds[6], 71), 0)
    right_root = draw_right_root(jax.random.fold_in(seeds[6], 71), 0)
    owner_table = draw_owner_table(jax.random.fold_in(seeds[6], 71), 0)
    return {"grad": grad, "left_factor": left_factor, "right_factor": right_factor, "left_root": left_root, "right_root": right_root, "owner_table": owner_table}


moment_decay = 0.9


def homes_of(owner_table):
    numbers = jnp.arange(NB, dtype=jnp.int32)
    same_owner = owner_table[:, None] == owner_table[None, :]
    before = numbers[None, :] < numbers[:, None]
    slot_of = jnp.sum((same_owner & before).astype(jnp.int32), axis=1).astype(jnp.int32)
    return (owner_table * MOST + slot_of).astype(jnp.int32)


def reference(grad, left_factor, right_factor, left_root, right_root, owner_table):
    home = homes_of(owner_table)
    highest = lax.Precision.HIGHEST
    weight = (1.0 - moment_decay) / BLK

    def one_block(block):
        target = home[block]
        matrix = grad[block]
        left_term = jnp.dot(matrix, matrix.T, precision=highest)
        right_term = jnp.dot(matrix.T, matrix, precision=highest)
        left_next = moment_decay * left_factor[target] + weight * left_term
        right_next = moment_decay * right_factor[target] + weight * right_term
        turned = jnp.dot(matrix, right_root[target], precision=highest)
        steered = jnp.dot(left_root[target], turned, precision=highest)
        return left_next, right_next, steered

    lefts, rights, direction = lax.map(one_block, jnp.arange(NB, dtype=jnp.int32))
    new_left = left_factor.at[home].set(lefts)
    new_right = right_factor.at[home].set(rights)
    return new_left, new_right, direction
```

```python
import functools

import jax
import jax.numpy as jnp
from jax import lax
from jax.experimental import pallas as pl
from jax.experimental.pallas import tpu as pltpu
from jax.sharding import PartitionSpec as P

moment_decay = 0.9
MESH = pl.DeviceIdType.MESH
bf16 = jnp.bfloat16
f32 = jnp.float32

NZ, NS, NX = 16, 8, 4
Z_IN, S_IN, X_A, X_B, X_FA, X_FB, S_OUT, Z_OUT, L_A, L_B, L_FA, L_FB = range(12)
C_G, C_R, C_LF, C_RF = range(4)


def split(x):
    hi = x.astype(bf16)
    return hi, (x - hi.astype(f32)).astype(bf16)


def dot3(a, b, dims):
    def one(p, q):
        return lax.dot_general(p, q, (dims, ((), ())), preferred_element_type=f32)

    return one(a[0], b[0]) + (one(a[0], b[1]) + one(a[1], b[0]))


def kernel(
    owner_ref, table_ref, grad_ref, lf_ref, rf_ref, lroot_ref, rroot_ref, live_ref,
    left_out, right_out, dir_out,
    gq, send, zin, gbuf, band, ghi, glo, lbuf, rr, lf, rf, dbuf, pout, rbuf,
    send_sem, recv_sem, loc_sem, in_sem,
):
    me, r = lax.axis_index("fsdp"), lax.axis_index("rep")
    z, s = lax.div(me, NS), lax.rem(me, NS)
    xa, xb = lax.rem(r + 1, NX), lax.rem(r + 3, NX)
    xc = lax.rem(r + 2, NX)

    def remote(src, dst, kind, k, dev):
        return pltpu.make_async_remote_copy(
            src_ref=src, dst_ref=dst, send_sem=send_sem.at[kind, k], recv_sem=recv_sem.at[kind, k],
            device_id=dev, device_id_type=MESH,
        )

    def wait_bytes(ref, sem):
        pltpu.make_async_copy(ref, ref, sem).wait()

    def zdev(d):
        zz = lax.rem(z + d, NZ)
        return zz, (zz * NS + s, r)

    def sdev(d):
        ss = lax.rem(s + d, NS)
        return ss, (z * NS + ss, r)

    def load(src, dst, i):
        c = pltpu.make_async_copy(src, dst, in_sem.at[i])
        c.start()
        return c

    cols = pl.ds(pl.multiple_of(r * 128, 128), 128)
    in_g = load(grad_ref.at[:, :, cols], gq, C_G)
    in_r = load(rroot_ref, rr, C_R)
    in_lf = load(lf_ref, lf, C_LF)
    in_rf = load(rf_ref, rf, C_RF)

    barrier = pltpu.get_barrier_semaphore()

    @pl.loop(1, NZ)
    def _(d):
        pl.semaphore_signal(barrier, inc=1, device_id=zdev(d)[1], device_id_type=MESH)

    @pl.loop(1, NS)
    def _(d):
        pl.semaphore_signal(barrier, inc=1, device_id=sdev(d)[1], device_id_type=MESH)

    for x in (xa, xb):
        pl.semaphore_signal(barrier, inc=1, device_id=(me, x), device_id_type=MESH)

    in_g.wait()

    def pack(k):
        @pl.loop(0, 128, unroll=8)
        def _(o):
            send[k, o] = gq[table_ref[k, o]]

    pack(0)
    pl.semaphore_wait(barrier, NZ - 1 + NS - 1 + 2)

    def z_in(k):
        @pl.loop(1, NZ)
        def _(d):
            zz, dev = zdev(d)
            remote(send.at[k, pl.ds(zz * NS, NS)], zin.at[k, z], Z_IN, k, dev).start()

        c = pltpu.make_async_copy(send.at[k, pl.ds(z * NS, NS)], zin.at[k, z], loc_sem.at[0, k])
        c.start()
        return c

    def x_pair(own, src, ka, kb, k):
        remote(src, own, ka, k, (me, xa)).start()
        remote(src, own, kb, k, (me, xb)).start()

    own_z = [None, None]
    own_z[0] = z_in(0)
    loc_l = []
    for k in range(2):
        x_pair(lbuf.at[r, k], lroot_ref.at[k], L_A, L_B, k)
        c = pltpu.make_async_copy(lroot_ref.at[k], lbuf.at[r, k], loc_sem.at[1, k])
        c.start()
        loc_l.append(c)
    pack(1)
    own_z[1] = z_in(1)

    def l_forward(k):
        wait_bytes(lbuf.at[xb, k], recv_sem.at[L_A, k])
        h = lbuf.at[xb, k, pl.ds(0, 64)]
        remote(h, h, L_FA, k, (me, xa)).start()
        wait_bytes(lbuf.at[xa, k], recv_sem.at[L_B, k])
        h = lbuf.at[xa, k, pl.ds(64, 64)]
        remote(h, h, L_FB, k, (me, xb)).start()

    def s_in(k):
        wait_bytes(zin.at[k, pl.ds(0, NZ - 1)], recv_sem.at[Z_IN, k])
        own_z[k].wait()

        @pl.loop(1, NS)
        def _(d):
            ss, dev = sdev(d)
            remote(zin.at[k, :, ss], gbuf.at[k, r, :, s], S_IN, k, dev).start()

        c = pltpu.make_async_copy(zin.at[k, :, s], gbuf.at[k, r, :, s], loc_sem.at[2, k])
        c.start()
        return c

    def x_start(k, own):
        wait_bytes(gbuf.at[k, r, :, pl.ds(0, NS - 1)], recv_sem.at[S_IN, k])
        own.wait()
        g = gbuf.at[k, r]
        x_pair(g, g, X_A, X_B, k)

    def take(k, q):
        @pl.loop(0, NZ)
        def _(zz):
            base = pl.multiple_of(zz * 32, 32)
            for ss in range(NS):
                band[pl.ds(base + ss * 4, 4), :] = gbuf[k, q, zz, ss]

        hi, lo = split(band[...])
        at = pl.ds(pl.multiple_of(q * 128, 128), 128)
        ghi[k, :, at] = hi
        glo[k, :, at] = lo

    def x_forward(k):
        wait_bytes(gbuf.at[k, xb], recv_sem.at[X_A, k])
        h = gbuf.at[k, xb, pl.ds(0, 8)]
        remote(h, h, X_FA, k, (me, xa)).start()
        wait_bytes(gbuf.at[k, xa], recv_sem.at[X_B, k])
        h = gbuf.at[k, xa, pl.ds(8, 8)]
        remote(h, h, X_FB, k, (me, xb)).start()

    def x_end(k):
        wait_bytes(gbuf.at[k, xc, pl.ds(0, 8)], recv_sem.at[X_FA, k])
        wait_bytes(gbuf.at[k, xc, pl.ds(8, 8)], recv_sem.at[X_FB, k])

    def steer(k):
        turned = dot3((ghi[k], glo[k]), split(rr[k]), ((1,), (1,)))
        t = split(turned)
        for q in range(NX):
            part = dot3(split(lbuf[q, k]), t, ((1,), (0,)))
            band[pl.ds(q * 128, 128), :] = part

        @pl.loop(0, NZ)
        def _(zz):
            base = pl.multiple_of(zz * 32, 32)
            for ss in range(NS):
                dbuf[k, zz, ss] = band[pl.ds(base + ss * 4, 4), :]

    def s_out(k):
        @pl.loop(1, NS)
        def _(d):
            ss, dev = sdev(d)
            remote(dbuf.at[k, :, ss], pout.at[k, :, s], S_OUT, k, dev).start()

        c = pltpu.make_async_copy(dbuf.at[k, :, s], pout.at[k, :, s], loc_sem.at[3, k])
        c.start()
        return c

    def z_out(k, own):
        wait_bytes(pout.at[k, :, pl.ds(0, NS - 1)], recv_sem.at[S_OUT, k])
        own.wait()

        @pl.loop(1, NZ)
        def _(d):
            zz, dev = zdev(d)
            remote(pout.at[k, zz], rbuf.at[k, z], Z_OUT, k, dev).start()

        c = pltpu.make_async_copy(pout.at[k, z], rbuf.at[k, z], loc_sem.at[4, k])
        c.start()
        return c

    weight = (1.0 - moment_decay) / 512
    rows = pl.ds(pl.multiple_of(r * 128, 128), 128)

    def stats(k):
        live = live_ref[k][:1, :1] > 0
        g = (ghi[k], glo[k])
        term = dot3((ghi[k, rows, :], glo[k, rows, :]), g, ((1,), (1,)))
        old = lf[k]
        left_out[k] = jnp.where(live, moment_decay * old + weight * term, old)
        term = dot3((ghi[k, :, rows], glo[k, :, rows]), g, ((0,), (0,)))
        old = rf[k]
        right_out[k] = jnp.where(live, moment_decay * old + weight * term, old)

    own0 = s_in(0)
    l_forward(0)
    x_start(0, own0)
    take(0, r)
    l_forward(1)
    own1 = s_in(1)
    x_forward(0)
    take(0, xb)
    take(0, xa)
    x_start(1, own1)
    take(1, r)
    in_r.wait()
    for k in range(2):
        loc_l[k].wait()
    for k in range(2):
        wait_bytes(lbuf.at[xc, k, pl.ds(0, 64)], recv_sem.at[L_FA, k])
        wait_bytes(lbuf.at[xc, k, pl.ds(64, 64)], recv_sem.at[L_FB, k])
    x_end(0)
    take(0, xc)
    steer(0)
    out0 = s_out(0)
    x_forward(1)
    in_lf.wait()
    in_rf.wait()
    fin0 = z_out(0, out0)
    take(1, xb)
    take(1, xa)
    x_end(1)
    take(1, xc)
    steer(1)
    out1 = s_out(1)
    stats(0)
    fin1 = z_out(1, out1)
    stats(1)
    fins = [fin0, fin1]
    for k in range(2):
        wait_bytes(rbuf.at[k, pl.ds(0, NZ - 1)], recv_sem.at[Z_OUT, k])
        fins[k].wait()

    @pl.loop(0, 128, unroll=8)
    def _(b):
        o = owner_ref[b]
        k = jnp.where(table_ref[0, o] == b, 0, 1)
        dir_out[b] = rbuf[k, lax.div(o, NS), lax.rem(o, NS)]

    for k in range(2):
        wait_bytes(zin.at[k, pl.ds(0, NZ - 1)], send_sem.at[Z_IN, k])
        wait_bytes(gbuf.at[k, r, :, pl.ds(0, NS - 1)], send_sem.at[S_IN, k])
        for kind in (X_A, X_B):
            wait_bytes(gbuf.at[k, r], send_sem.at[kind, k])
        for kind in (X_FA, X_FB):
            wait_bytes(gbuf.at[k, r, pl.ds(0, 8)], send_sem.at[kind, k])
        for kind in (L_A, L_B):
            wait_bytes(lbuf.at[r, k], send_sem.at[kind, k])
        for kind in (L_FA, L_FB):
            wait_bytes(lbuf.at[r, k, pl.ds(0, 64)], send_sem.at[kind, k])
        wait_bytes(pout.at[k, :, pl.ds(0, NS - 1)], send_sem.at[S_OUT, k])
        wait_bytes(rbuf.at[k, pl.ds(0, NZ - 1)], send_sem.at[Z_OUT, k])


def body(grad, left_factor, right_factor, left_root, right_root, owner_table):
    numbers = jnp.arange(128, dtype=jnp.int32)
    match = owner_table[None, :] == numbers[:, None]
    first = jnp.min(jnp.where(match, numbers[None, :], 128), axis=1)
    last = jnp.max(jnp.where(match, numbers[None, :], -1), axis=1)
    table = jnp.stack([jnp.minimum(first, 127), jnp.maximum(last, 0)])
    me = lax.axis_index("fsdp")
    mine = jnp.stack([lax.dynamic_index_in_dim(first, me, 0, False), lax.dynamic_index_in_dim(last, me, 0, False)])
    live = jnp.stack([mine[0] < 128, mine[1] > mine[0]])
    live = jnp.broadcast_to(live.astype(jnp.int32)[:, None, None], (2, 8, 128))

    any_spec = pl.BlockSpec(memory_space=pl.ANY)
    vmem = pl.BlockSpec(memory_space=pltpu.VMEM)
    smem = pl.BlockSpec(memory_space=pltpu.SMEM)
    piece = (NZ, NS, 4, 128)
    return pl.pallas_call(
        kernel,
        out_shape=(
            jax.ShapeDtypeStruct((2, 128, 512), f32),
            jax.ShapeDtypeStruct((2, 128, 512), f32),
            jax.ShapeDtypeStruct((128, 4, 128), f32),
        ),
        in_specs=[smem, smem] + [any_spec] * 5 + [vmem],
        out_specs=(vmem, vmem, vmem),
        scratch_shapes=[
            pltpu.VMEM((128, 4, 128), f32),
            pltpu.VMEM((2, 128, 4, 128), f32),
            pltpu.VMEM((2,) + piece, f32),
            pltpu.VMEM((2, NX) + piece, f32),
            pltpu.VMEM((512, 128), f32),
            pltpu.VMEM((2, 512, 512), bf16),
            pltpu.VMEM((2, 512, 512), bf16),
            pltpu.VMEM((NX, 2, 128, 512), f32),
            pltpu.VMEM((2, 128, 512), f32),
            pltpu.VMEM((2, 128, 512), f32),
            pltpu.VMEM((2, 128, 512), f32),
            pltpu.VMEM((2,) + piece, f32),
            pltpu.VMEM((2,) + piece, f32),
            pltpu.VMEM((2,) + piece, f32),
            pltpu.SemaphoreType.DMA((12, 2)),
            pltpu.SemaphoreType.DMA((12, 2)),
            pltpu.SemaphoreType.DMA((5, 2)),
            pltpu.SemaphoreType.DMA((4,)),
        ],
        compiler_params=pltpu.CompilerParams(
            collective_id=0, has_side_effects=True, vmem_limit_bytes=40 * 1024 * 1024
        ),
        cost_estimate=pl.CostEstimate(flops=1610612736, bytes_accessed=4500000, transcendentals=0),
    )(owner_table, table, grad, left_factor, right_factor, left_root, right_root, live)


def solution(mesh):
    placed = (
        P(None, "fsdp", None),
        P("fsdp", "rep", None),
        P("fsdp", "rep", None),
        P("fsdp", "rep", None),
        P("fsdp", "rep", None),
        P(),
    )
    return jax.shard_map(
        body,
        mesh=mesh,
        in_specs=placed,
        out_specs=(P("fsdp", "rep", None), P("fsdp", "rep", None), P(None, "fsdp", "rep")),
        check_vma=False,
    )
```

```python
import jax
import jax.numpy as jnp
from jax import lax
from jax.experimental import pallas as pl
from jax.experimental.pallas import tpu as pltpu
from jax.sharding import PartitionSpec as P

moment_decay = 0.9
MESH = pl.DeviceIdType.MESH
bf16 = jnp.bfloat16
f32 = jnp.float32
i32 = jnp.int32

NF, NX = 128, 4
IN, OUT, XA0, XA1, XB0, XB1, XFA, XFB, LA, LB, LFA, LFB = range(12)


def split(x):
    hi = x.astype(bf16)
    return hi, (x - hi.astype(f32)).astype(bf16)


def dot3(a, b, dims):
    def one(p, q):
        return lax.dot_general(p, q, (dims, ((), ())), preferred_element_type=f32)

    return one(a[0], b[0]) + (one(a[0], b[1]) + one(a[1], b[0]))


def kernel(
    owner_ref, row_ref, grad_ref, lf_ref, rf_ref, lroot_ref, rroot_ref,
    left_out, right_out, dir_out,
    gq, send, gbuf, band, ghi, glo, lown, lbuf, lhi, llo, rr, lf, rf, dbuf, rbuf,
    left_new, right_new, dir_new, tab_v, tab_s,
    send_sem, recv_sem, loc_sem, in_sem, out_sem,
):
    me, r = lax.axis_index("fsdp"), lax.axis_index("rep")
    chip, core = lax.div(me, 2), lax.rem(me, 2)
    xa, xb, xc = lax.rem(r + 1, NX), lax.rem(r + 3, NX), lax.rem(r + 2, NX)

    def at128(q):
        return pl.ds(pl.multiple_of(q * 128, 128), 128)

    def load(src, dst, i):
        c = pltpu.make_async_copy(src, dst, in_sem.at[i])
        c.start()
        return c

    in_g = load(grad_ref.at[:, :, at128(r)], gq, 0)
    in_l = load(lroot_ref, lown, 1)
    in_r = load(rroot_ref, rr, 2)
    in_lf = load(lf_ref, lf, 3)
    in_rf = load(rf_ref, rf, 4)

    barrier = pltpu.get_barrier_semaphore()

    @pl.loop(1, NF)
    def _(d):
        pl.semaphore_signal(barrier, inc=1, device_id=(lax.rem(me + d, NF), r), device_id_type=MESH)

    for x in (xa, xb):
        pl.semaphore_signal(barrier, inc=1, device_id=(me, x), device_id_type=MESH)

    owner_of = jnp.transpose(jnp.broadcast_to(row_ref[...], (NF, NF)))
    block = lax.broadcasted_iota(i32, (NF, NF), 0)
    lane = lax.broadcasted_iota(i32, (NF, NF), 1)
    match = owner_of == lane
    first = jnp.min(jnp.where(match, block, NF), axis=0, keepdims=True)
    last = jnp.max(jnp.where(match, block, -1), axis=0, keepdims=True)
    tab_v[0:1, :] = jnp.minimum(first, NF - 1)
    tab_v[1:2, :] = jnp.maximum(last, 0)
    to_s = pltpu.make_async_copy(tab_v, tab_s, loc_sem.at[2, 0])
    to_s.start()
    mine = lane[:1, :] == me
    live0 = jnp.max(jnp.where(mine & (first < NF), 1, 0), axis=1, keepdims=True)
    live1 = jnp.max(jnp.where(mine & (last > first), 1, 0), axis=1, keepdims=True)
    live = (live0, live1)

    def remote(src, dst, kind, k, dev):
        return pltpu.make_async_remote_copy(
            src_ref=src, dst_ref=dst, send_sem=send_sem.at[kind, k], recv_sem=recv_sem.at[kind, k],
            device_id=dev, device_id_type=MESH,
        )

    def wait_bytes(ref, sem):
        pltpu.make_async_copy(ref, ref, sem).wait()

    to_a, to_b = (me, xa), (me, xb)

    to_s.wait()
    in_g.wait()

    def pack(k):
        @pl.loop(0, NF, unroll=8)
        def _(o):
            send[k, o] = gq[tab_s[k, o]]

    pack(0)
    pl.semaphore_wait(barrier, NF - 1 + 2)

    def send_in(k, cc):
        def piece(o):
            remote(send.at[k, o], gbuf.at[k, r, me], IN, k, (o, r)).start()

        @pl.when(core != cc)
        def _():
            piece(chip * 2 + cc)

        @pl.loop(1, NF // 2)
        def _(j):
            piece(lax.rem(chip + j, NF // 2) * 2 + cc)

    def own_copy(src, dst, i, k):
        c = pltpu.make_async_copy(src, dst, loc_sem.at[i, k])
        c.start()
        return c

    own_in = [None, None]
    send_in(0, 0)
    in_l.wait()

    def l_start(k):
        def block_to(q, slot, kind, dev):
            remote(lown.at[k, :, at128(q)], lbuf.at[k, slot], kind, k, dev).start()

        block_to(r, 0, LA, to_b)
        block_to(r, 3, LB, to_a)
        block_to(xa, 1, LA, to_b)
        block_to(xb, 4, LB, to_a)
        if k == 0:
            block_to(xc, 2, LA, to_b)
        else:
            block_to(xc, 2, LB, to_a)

    l_start(0)
    send_in(0, 1)
    own_in[0] = own_copy(send.at[0, me], gbuf.at[0, r, me], 0, 0)
    l_start(1)
    pack(1)
    send_in(1, 0)
    send_in(1, 1)
    own_in[1] = own_copy(send.at[1, me], gbuf.at[1, r, me], 0, 1)

    from_a = (pl.ds(0, 3), pl.ds(0, 2))
    from_b = (pl.ds(3, 2), pl.ds(2, 3))

    def l_forward(k):
        wait_bytes(lbuf.at[k, from_a[k]], recv_sem.at[LA, k])
        remote(lbuf.at[k, 0, pl.ds(0, 64)], lbuf.at[k, 5, pl.ds(0, 64)], LFA, k, to_b).start()
        wait_bytes(lbuf.at[k, from_b[k]], recv_sem.at[LB, k])
        remote(lbuf.at[k, 3, pl.ds(64, 64)], lbuf.at[k, 5, pl.ds(64, 64)], LFB, k, to_a).start()

    def l_put(k, p, q, x):
        hi, lo = split(x)
        lhi[k, at128(p), at128(q)] = hi
        llo[k, at128(p), at128(q)] = lo

    def l_both(k, p, q, x):
        l_put(k, p, q, x)
        l_put(k, q, p, jnp.transpose(x))

    def l_own(k):
        l_put(k, r, r, lown[k, :, at128(r)])
        for q in (xa, xb, xc):
            l_both(k, r, q, lown[k, :, at128(q)])

    def l_take(k):
        l_put(k, xa, xa, lbuf[k, 0])
        l_both(k, xa, xc, lbuf[k, 1])
        if k == 0:
            l_both(k, xa, xb, lbuf[k, 2])
        else:
            l_both(k, xb, xa, lbuf[k, 2])
        l_put(k, xb, xb, lbuf[k, 3])
        l_both(k, xb, xc, lbuf[k, 4])

    def l_end(k):
        wait_bytes(lbuf.at[k, 5, pl.ds(0, 64)], recv_sem.at[LFA, k])
        wait_bytes(lbuf.at[k, 5, pl.ds(64, 64)], recv_sem.at[LFB, k])
        l_put(k, xc, xc, lbuf[k, 5])

    low, high = pl.ds(0, NF // 2), pl.ds(NF // 2, NF // 2)

    def x_start(k):
        wait_bytes(gbuf.at[k, r, pl.ds(0, NF - 1)], recv_sem.at[IN, k])
        own_in[k].wait()
        g0, g1 = gbuf.at[k, r, low], gbuf.at[k, r, high]
        remote(g0, g0, XA0, k, to_a).start()
        remote(g1, g1, XB1, k, to_b).start()
        remote(g1, g1, XA1, k, to_a).start()
        remote(g0, g0, XB0, k, to_b).start()

    def x_forward(k):
        g = gbuf.at[k, xb, low]
        wait_bytes(g, recv_sem.at[XA0, k])
        remote(g, g, XFA, k, to_a).start()
        g = gbuf.at[k, xa, high]
        wait_bytes(g, recv_sem.at[XB1, k])
        remote(g, g, XFB, k, to_b).start()

    def take(k, q):
        @pl.loop(0, 16)
        def _(i):
            for j in range(8):
                band[pl.ds(pl.multiple_of(i * 32, 32) + j * 4, 4), :] = gbuf[k, q, i * 8 + j]

        hi, lo = split(band[...])
        ghi[k, :, at128(q)] = hi
        glo[k, :, at128(q)] = lo

    def x_take(k):
        wait_bytes(gbuf.at[k, xb, high], recv_sem.at[XA1, k])
        take(k, xb)
        wait_bytes(gbuf.at[k, xa, low], recv_sem.at[XB0, k])
        take(k, xa)
        wait_bytes(gbuf.at[k, xc, low], recv_sem.at[XFA, k])
        wait_bytes(gbuf.at[k, xc, high], recv_sem.at[XFB, k])
        take(k, xc)

    def steer(k):
        turned = dot3((ghi[k], glo[k]), split(rr[k]), ((1,), (1,)))
        band[...] = dot3((lhi[k], llo[k]), split(turned), ((1,), (0,)))

        @pl.loop(0, 16)
        def _(i):
            for j in range(8):
                dbuf[k, i * 8 + j] = band[pl.ds(pl.multiple_of(i * 32, 32) + j * 4, 4), :]

    def send_out(k):
        @pl.loop(1, NF)
        def _(d):
            f = lax.rem(me + d, NF)
            remote(dbuf.at[k, f], rbuf.at[k, me], OUT, k, (f, r)).start()

        return own_copy(dbuf.at[k, me], rbuf.at[k, me], 1, k)

    weight = (1.0 - moment_decay) / 512

    def stats(k):
        g = (ghi[k], glo[k])
        term = dot3((ghi[k, at128(r), :], glo[k, at128(r), :]), g, ((1,), (1,)))
        old = lf[k]
        left_new[k] = jnp.where(live[k] > 0, moment_decay * old + weight * term, old)
        term = dot3((ghi[k, :, at128(r)], glo[k, :, at128(r)]), g, ((0,), (0,)))
        old = rf[k]
        right_new[k] = jnp.where(live[k] > 0, moment_decay * old + weight * term, old)

    l_own(0)
    l_own(1)
    l_forward(0)
    l_take(0)
    l_forward(1)
    x_start(0)
    take(0, r)
    x_forward(0)
    l_take(1)
    l_end(0)
    in_r.wait()
    x_take(0)
    steer(0)
    own_out0 = send_out(0)
    l_end(1)
    x_start(1)
    take(1, r)
    x_forward(1)
    x_take(1)
    steer(1)
    own_out1 = send_out(1)
    in_lf.wait()
    in_rf.wait()
    stats(0)
    stats(1)
    out_l = pltpu.make_async_copy(left_new, left_out, out_sem.at[0])
    out_l.start()
    out_r = pltpu.make_async_copy(right_new, right_out, out_sem.at[1])
    out_r.start()

    own_outs = (own_out0, own_out1)
    for k in range(2):
        wait_bytes(rbuf.at[k, pl.ds(0, NF - 1)], recv_sem.at[OUT, k])
        own_outs[k].wait()

    @pl.loop(0, NF, unroll=8)
    def _(b):
        o = owner_ref[b]
        dir_new[b] = rbuf[jnp.where(tab_s[0, o] == b, 0, 1), o]

    out_d = pltpu.make_async_copy(dir_new, dir_out, out_sem.at[2])
    out_d.start()
    for k in range(2):
        wait_bytes(gbuf.at[k, r, pl.ds(0, NF - 1)], send_sem.at[IN, k])
        wait_bytes(rbuf.at[k, pl.ds(0, NF - 1)], send_sem.at[OUT, k])
        for kind in (XA0, XA1, XB0, XB1, XFA, XFB):
            wait_bytes(gbuf.at[k, r, low], send_sem.at[kind, k])
        wait_bytes(lbuf.at[k, from_a[k]], send_sem.at[LA, k])
        wait_bytes(lbuf.at[k, from_b[k]], send_sem.at[LB, k])
        for kind in (LFA, LFB):
            wait_bytes(lbuf.at[k, 5, pl.ds(0, 64)], send_sem.at[kind, k])
    out_l.wait()
    out_r.wait()
    out_d.wait()


def body(grad, left_factor, right_factor, left_root, right_root, owner_table):
    hbm = pl.BlockSpec(memory_space=pltpu.HBM)
    vmem = pl.BlockSpec(memory_space=pltpu.VMEM)
    smem = pl.BlockSpec(memory_space=pltpu.SMEM)
    pieces = (2, NF, 4, 128)
    return pl.pallas_call(
        kernel,
        out_shape=(
            jax.ShapeDtypeStruct((2, 128, 512), f32),
            jax.ShapeDtypeStruct((2, 128, 512), f32),
            jax.ShapeDtypeStruct((NF, 4, 128), f32),
        ),
        in_specs=[smem, vmem] + [hbm] * 5,
        out_specs=(hbm, hbm, hbm),
        scratch_shapes=[
            pltpu.VMEM((NF, 4, 128), f32),
            pltpu.VMEM(pieces, f32),
            pltpu.VMEM((2, NX, NF, 4, 128), f32),
            pltpu.VMEM((512, 128), f32),
            pltpu.VMEM((2, 512, 512), bf16),
            pltpu.VMEM((2, 512, 512), bf16),
            pltpu.VMEM((2, 128, 512), f32),
            pltpu.VMEM((2, 6, 128, 128), f32),
            pltpu.VMEM((2, 512, 512), bf16),
            pltpu.VMEM((2, 512, 512), bf16),
            pltpu.VMEM((2, 128, 512), f32),
            pltpu.VMEM((2, 128, 512), f32),
            pltpu.VMEM((2, 128, 512), f32),
            pltpu.VMEM(pieces, f32),
            pltpu.VMEM(pieces, f32),
            pltpu.VMEM((2, 128, 512), f32),
            pltpu.VMEM((2, 128, 512), f32),
            pltpu.VMEM((NF, 4, 128), f32),
            pltpu.VMEM((8, 128), i32),
            pltpu.SMEM((8, 128), i32),
            pltpu.SemaphoreType.DMA((12, 2)),
            pltpu.SemaphoreType.DMA((12, 2)),
            pltpu.SemaphoreType.DMA((3, 2)),
            pltpu.SemaphoreType.DMA((5,)),
            pltpu.SemaphoreType.DMA((3,)),
        ],
        compiler_params=pltpu.CompilerParams(
            collective_id=0, has_side_effects=True, vmem_limit_bytes=56 * 1024 * 1024
        ),
        cost_estimate=pl.CostEstimate(flops=1610612736, bytes_accessed=4500000, transcendentals=0),
    )(owner_table, owner_table.reshape(1, NF), grad, left_factor, right_factor, left_root, right_root)


def solution(mesh):
    placed = (
        P(None, "fsdp", None),
        P("fsdp", "rep", None),
        P("fsdp", "rep", None),
        P("fsdp", "rep", None),
        P("fsdp", "rep", None),
        P(),
    )
    return jax.shard_map(
        body,
        mesh=mesh,
        in_specs=placed,
        out_specs=(P("fsdp", "rep", None), P("fsdp", "rep", None), P(None, "fsdp", "rep")),
        check_vma=False,
    )
```

```python
import jax
import jax.numpy as jnp
from jax import lax
from jax.experimental import pallas as pl
from jax.experimental.pallas import tpu as pltpu
from jax.sharding import PartitionSpec as P

moment_decay = 0.9
MESH = pl.DeviceIdType.MESH
bf16 = jnp.bfloat16
f32 = jnp.float32
i32 = jnp.int32

NF, NX = 128, 4
IN0, IN1, OUT, LA, LB, LFA, LFB = range(7)
XA0, XA1, XB0, XB1, XFA, XFB = range(6)


def split(x):
    hi = x.astype(bf16)
    return hi, (x - hi.astype(f32)).astype(bf16)


def dot3(a, b, dims):
    def one(p, q):
        return lax.dot_general(p, q, (dims, ((), ())), preferred_element_type=f32)

    return one(a[0], b[0]) + (one(a[0], b[1]) + one(a[1], b[0]))


def kernel(
    owner_ref, row_ref, grad_ref, lf_ref, rf_ref, lroot_ref, rroot_ref,
    left_out, right_out, dir_out,
    gq, send, gbuf, band, acc, ghi, glo, lown, lbuf, lhi, llo, rr, rhi, rlo, lf, rf, dbuf, rbuf,
    left_new, right_new, dir_new, tab_v, tab_s,
    send_sem, recv_sem, x_send_sem, x_recv_sem, loc_sem, in_sem, out_sem,
):
    me, r = lax.axis_index("fsdp"), lax.axis_index("rep")
    chip, core = lax.div(me, 2), lax.rem(me, 2)
    xa, xb, xc = lax.rem(r + 1, NX), lax.rem(r + 3, NX), lax.rem(r + 2, NX)

    def at128(q):
        return pl.ds(pl.multiple_of(q * 128, 128), 128)

    def load(src, dst, i):
        c = pltpu.make_async_copy(src, dst, in_sem.at[i])
        c.start()
        return c

    in_g = load(grad_ref.at[:, :, at128(r)], gq, 0)
    in_l = load(lroot_ref, lown, 1)
    in_r = load(rroot_ref, rr, 2)
    in_lf = load(lf_ref, lf, 3)
    in_rf = load(rf_ref, rf, 4)

    barrier = pltpu.get_barrier_semaphore()

    @pl.loop(0, NF // 8)
    def _(t):
        far = NF // 16 + lax.div(t + 1, 2) * (1 - 2 * lax.rem(t, 2))
        for i in range(8):
            f = lax.rem(me + far * 8 + i, NF)

            @pl.when(f != me)
            def _():
                pl.semaphore_signal(barrier, inc=1, device_id=(f, r), device_id_type=MESH)

    for x in (xa, xb):
        pl.semaphore_signal(barrier, inc=1, device_id=(me, x), device_id_type=MESH)

    owner_of = jnp.transpose(jnp.broadcast_to(row_ref[...], (NF, NF)))
    block = lax.broadcasted_iota(i32, (NF, NF), 0)
    lane = lax.broadcasted_iota(i32, (NF, NF), 1)
    match = owner_of == lane
    first = jnp.min(jnp.where(match, block, NF), axis=0, keepdims=True)
    last = jnp.max(jnp.where(match, block, -1), axis=0, keepdims=True)
    tab_v[0:1, :] = jnp.minimum(first, NF - 1)
    tab_v[1:2, :] = jnp.maximum(last, 0)
    to_s = pltpu.make_async_copy(tab_v, tab_s, loc_sem.at[2, 0])
    to_s.start()
    mine = lane[:1, :] == me
    live0 = jnp.max(jnp.where(mine & (first < NF), 1, 0), axis=1, keepdims=True)
    live1 = jnp.max(jnp.where(mine & (last > first), 1, 0), axis=1, keepdims=True)
    live = (live0, live1)

    def remote(src, dst, kind, k, dev):
        return pltpu.make_async_remote_copy(
            src_ref=src, dst_ref=dst, send_sem=send_sem.at[kind, k], recv_sem=recv_sem.at[kind, k],
            device_id=dev, device_id_type=MESH,
        )

    def wait_bytes(ref, sem):
        pltpu.make_async_copy(ref, ref, sem).wait()

    to_a, to_b = (me, xa), (me, xb)

    to_s.wait()
    in_g.wait()

    def pack(k):
        @pl.loop(0, NF, unroll=8)
        def _(o):
            send[k, o] = gq[tab_s[k, o]]

    pack(0)
    pl.semaphore_wait(barrier, NF - 1 + 2)

    def send_in(k, cc):
        @pl.when(core != cc)
        def _():
            o = chip * 2 + cc
            remote(send.at[k, o], gbuf.at[k, r, core], IN1, k, (o, r)).start()

        def piece(j, kind):
            o = lax.rem(chip + j, NF // 2) * 2 + cc
            remote(send.at[k, o], gbuf.at[k, r, (NF // 2 - j) * 2 + core], kind, k, (o, r)).start()

        @pl.loop(1, 33)
        def _(j):
            piece(j, IN0)

        @pl.loop(33, NF // 2)
        def _(j):
            piece(j, IN1)

    def own_copy(src, dst, i, k):
        c = pltpu.make_async_copy(src, dst, loc_sem.at[i, k])
        c.start()
        return c

    own_in = [None, None]
    send_in(0, 0)
    in_l.wait()

    def l_start(k):
        def block_to(q, slot, kind, dev):
            remote(lown.at[k, :, at128(q)], lbuf.at[k, slot], kind, k, dev).start()

        block_to(r, 0, LA, to_b)
        block_to(r, 3, LB, to_a)
        block_to(xa, 1, LA, to_b)
        block_to(xb, 4, LB, to_a)
        if k == 0:
            block_to(xc, 2, LA, to_b)
        else:
            block_to(xc, 2, LB, to_a)

    l_start(0)
    send_in(0, 1)
    own_in[0] = own_copy(send.at[0, me], gbuf.at[0, r, core], 0, 0)
    l_start(1)
    pack(1)
    send_in(1, 0)
    send_in(1, 1)
    own_in[1] = own_copy(send.at[1, me], gbuf.at[1, r, core], 0, 1)

    from_a = (pl.ds(0, 3), pl.ds(0, 2))
    from_b = (pl.ds(3, 2), pl.ds(2, 3))

    def l_forward(k):
        wait_bytes(lbuf.at[k, from_a[k]], recv_sem.at[LA, k])
        remote(lbuf.at[k, 0, pl.ds(0, 64)], lbuf.at[k, 5, pl.ds(0, 64)], LFA, k, to_b).start()
        wait_bytes(lbuf.at[k, from_b[k]], recv_sem.at[LB, k])
        remote(lbuf.at[k, 3, pl.ds(64, 64)], lbuf.at[k, 5, pl.ds(64, 64)], LFB, k, to_a).start()

    def l_put(k, p, q, x):
        hi, lo = split(x)
        lhi[k, at128(p), at128(q)] = hi
        llo[k, at128(p), at128(q)] = lo

    def l_both(k, p, q, x):
        l_put(k, p, q, x)
        l_put(k, q, p, jnp.transpose(x))

    def l_own(k):
        l_put(k, r, r, lown[k, :, at128(r)])
        for q in (xa, xb, xc):
            l_both(k, r, q, lown[k, :, at128(q)])

    def l_take(k):
        l_put(k, xa, xa, lbuf[k, 0])
        l_both(k, xa, xc, lbuf[k, 1])
        if k == 0:
            l_both(k, xa, xb, lbuf[k, 2])
        else:
            l_both(k, xb, xa, lbuf[k, 2])
        l_put(k, xb, xb, lbuf[k, 3])
        l_both(k, xb, xc, lbuf[k, 4])

    def l_end(k):
        wait_bytes(lbuf.at[k, 5, pl.ds(0, 64)], recv_sem.at[LFA, k])
        wait_bytes(lbuf.at[k, 5, pl.ds(64, 64)], recv_sem.at[LFB, k])
        l_put(k, xc, xc, lbuf[k, 5])

    half_at = (64, 0)

    def quarters(k, q, h):
        return gbuf.at[k, q, pl.ds(half_at[h], 32)], gbuf.at[k, q, pl.ds(half_at[h] + 32, 32)]

    def x_remote(ref, kind, k, h, dev):
        pltpu.make_async_remote_copy(
            src_ref=ref, dst_ref=ref, send_sem=x_send_sem.at[kind, k, h], recv_sem=x_recv_sem.at[kind, k, h],
            device_id=dev, device_id_type=MESH,
        ).start()

    def x_start(k, h):
        if h == 0:
            wait_bytes(gbuf.at[k, r, pl.ds(64, 64)], recv_sem.at[IN0, k])
        else:
            wait_bytes(gbuf.at[k, r, pl.ds(0, 63)], recv_sem.at[IN1, k])
            own_in[k].wait()
        g0, g1 = quarters(k, r, h)
        x_remote(g0, XA0, k, h, to_a)
        x_remote(g1, XB1, k, h, to_b)
        x_remote(g1, XA1, k, h, to_a)
        x_remote(g0, XB0, k, h, to_b)

    def x_forward(k, h):
        g0, _ = quarters(k, xb, h)
        wait_bytes(g0, x_recv_sem.at[XA0, k, h])
        x_remote(g0, XFA, k, h, to_a)
        _, g1 = quarters(k, xa, h)
        wait_bytes(g1, x_recv_sem.at[XB1, k, h])
        x_remote(g1, XFB, k, h, to_b)

    def take(k, q, start=False):
        @pl.loop(0, 8)
        def _(i):
            for j in range(8):
                m = i * 8 + j
                base = pl.multiple_of(lax.rem(chip + m, NF // 2) * 8, 8)
                band[pl.ds(base, 4), :] = gbuf[k, q, 2 * m]
                band[pl.ds(base + 4, 4), :] = gbuf[k, q, 2 * m + 1]

        g = split(band[...])
        ghi[k, :, at128(q)], glo[k, :, at128(q)] = g
        part = dot3(g, (rhi[k, at128(q), :], rlo[k, at128(q), :]), ((1,), (0,)))
        if start:
            acc[...] = part
        else:
            acc[...] += part

    def x_take(k):
        for h in range(2):
            _, g1 = quarters(k, xb, h)
            wait_bytes(g1, x_recv_sem.at[XA1, k, h])
        take(k, xb)
        for h in range(2):
            g0, _ = quarters(k, xa, h)
            wait_bytes(g0, x_recv_sem.at[XB0, k, h])
        take(k, xa)
        for h in range(2):
            g0, g1 = quarters(k, xc, h)
            wait_bytes(g0, x_recv_sem.at[XFA, k, h])
            wait_bytes(g1, x_recv_sem.at[XFB, k, h])
        take(k, xc)

    def steer_and_send(k):
        t = split(acc[...])

        @pl.loop(0, 4)
        def _(i):
            p = lax.rem(lax.div(chip, 16) + i, 4)
            band[pl.ds(0, 128), :] = dot3((lhi[k, at128(p), :], llo[k, at128(p), :]), t, ((1,), (0,)))
            for j in range(32):
                dbuf[k, p * 32 + j] = band[pl.ds(j * 4, 4), :]

            @pl.loop(0, 32)
            def _(j):
                f = p * 32 + lax.rem(me + j, 32)

                @pl.when(f != me)
                def _():
                    remote(dbuf.at[k, f], rbuf.at[k, me], OUT, k, (f, r)).start()

        return own_copy(dbuf.at[k, me], rbuf.at[k, me], 1, k)

    weight = (1.0 - moment_decay) / 512

    def stats(k):
        g = (ghi[k], glo[k])
        term = dot3((ghi[k, at128(r), :], glo[k, at128(r), :]), g, ((1,), (1,)))
        old = lf[k]
        left_new[k] = jnp.where(live[k] > 0, moment_decay * old + weight * term, old)
        term = dot3((ghi[k, :, at128(r)], glo[k, :, at128(r)]), g, ((0,), (0,)))
        old = rf[k]
        right_new[k] = jnp.where(live[k] > 0, moment_decay * old + weight * term, old)

    l_own(0)
    l_own(1)
    in_r.wait()
    for k in range(2):
        rhi[k], rlo[k] = split(jnp.transpose(rr[k]))
    l_forward(0)
    l_take(0)
    x_start(0, 0)
    x_start(0, 1)
    take(0, r, True)
    x_forward(0, 0)
    l_forward(1)
    x_forward(0, 1)
    l_end(0)
    x_take(0)
    own_out0 = steer_and_send(0)
    l_take(1)
    l_end(1)
    x_start(1, 0)
    x_start(1, 1)
    take(1, r, True)
    x_forward(1, 0)
    x_forward(1, 1)
    x_take(1)
    own_out1 = steer_and_send(1)
    in_lf.wait()
    in_rf.wait()
    stats(0)
    stats(1)
    out_l = pltpu.make_async_copy(left_new, left_out, out_sem.at[0])
    out_l.start()
    out_r = pltpu.make_async_copy(right_new, right_out, out_sem.at[1])
    out_r.start()

    own_outs = (own_out0, own_out1)
    for k in range(2):
        wait_bytes(rbuf.at[k, pl.ds(0, NF - 1)], recv_sem.at[OUT, k])
        own_outs[k].wait()

    @pl.loop(0, NF, unroll=8)
    def _(b):
        o = owner_ref[b]
        dir_new[b] = rbuf[jnp.where(tab_s[0, o] == b, 0, 1), o]

    out_d = pltpu.make_async_copy(dir_new, dir_out, out_sem.at[2])
    out_d.start()
    for k in range(2):
        wait_bytes(gbuf.at[k, r, pl.ds(64, 64)], send_sem.at[IN0, k])
        wait_bytes(gbuf.at[k, r, pl.ds(0, 63)], send_sem.at[IN1, k])
        wait_bytes(rbuf.at[k, pl.ds(0, NF - 1)], send_sem.at[OUT, k])
        for kind in (XA0, XA1, XB0, XB1, XFA, XFB):
            for h in range(2):
                wait_bytes(gbuf.at[k, r, pl.ds(0, 32)], x_send_sem.at[kind, k, h])
        wait_bytes(lbuf.at[k, from_a[k]], send_sem.at[LA, k])
        wait_bytes(lbuf.at[k, from_b[k]], send_sem.at[LB, k])
        for kind in (LFA, LFB):
            wait_bytes(lbuf.at[k, 5, pl.ds(0, 64)], send_sem.at[kind, k])
    out_l.wait()
    out_r.wait()
    out_d.wait()


def copy_out(a, b, c, a_out, b_out, c_out, sem):
    copies = [
        pltpu.make_async_copy(src, dst, sem.at[i])
        for i, (src, dst) in enumerate(((a, a_out), (b, b_out), (c, c_out)))
    ]
    for c in copies:
        c.start()
    for c in copies:
        c.wait()


def body(grad, left_factor, right_factor, left_root, right_root, owner_table):
    hbm = pl.BlockSpec(memory_space=pltpu.HBM)
    vmem = pl.BlockSpec(memory_space=pltpu.VMEM)
    smem = pl.BlockSpec(memory_space=pltpu.SMEM)
    pieces = (2, NF, 4, 128)
    results = pl.pallas_call(
        kernel,
        out_shape=(
            jax.ShapeDtypeStruct((2, 128, 512), f32),
            jax.ShapeDtypeStruct((2, 128, 512), f32),
            jax.ShapeDtypeStruct((NF, 4, 128), f32),
        ),
        in_specs=[smem, vmem] + [hbm] * 5,
        out_specs=(hbm, hbm, hbm),
        scratch_shapes=[
            pltpu.VMEM((NF, 4, 128), f32),
            pltpu.VMEM(pieces, f32),
            pltpu.VMEM((2, NX, NF, 4, 128), f32),
            pltpu.VMEM((512, 128), f32),
            pltpu.VMEM((512, 128), f32),
            pltpu.VMEM((2, 512, 512), bf16),
            pltpu.VMEM((2, 512, 512), bf16),
            pltpu.VMEM((2, 128, 512), f32),
            pltpu.VMEM((2, 6, 128, 128), f32),
            pltpu.VMEM((2, 512, 512), bf16),
            pltpu.VMEM((2, 512, 512), bf16),
            pltpu.VMEM((2, 128, 512), f32),
            pltpu.VMEM((2, 512, 128), bf16),
            pltpu.VMEM((2, 512, 128), bf16),
            pltpu.VMEM((2, 128, 512), f32),
            pltpu.VMEM((2, 128, 512), f32),
            pltpu.VMEM(pieces, f32),
            pltpu.VMEM(pieces, f32),
            pltpu.VMEM((2, 128, 512), f32),
            pltpu.VMEM((2, 128, 512), f32),
            pltpu.VMEM((NF, 4, 128), f32),
            pltpu.VMEM((8, 128), i32),
            pltpu.SMEM((8, 128), i32),
            pltpu.SemaphoreType.DMA((7, 2)),
            pltpu.SemaphoreType.DMA((7, 2)),
            pltpu.SemaphoreType.DMA((6, 2, 2)),
            pltpu.SemaphoreType.DMA((6, 2, 2)),
            pltpu.SemaphoreType.DMA((3, 2)),
            pltpu.SemaphoreType.DMA((5,)),
            pltpu.SemaphoreType.DMA((3,)),
        ],
        compiler_params=pltpu.CompilerParams(
            collective_id=0, has_side_effects=True, vmem_limit_bytes=56 * 1024 * 1024
        ),
        cost_estimate=pl.CostEstimate(flops=1610612736, bytes_accessed=4500000, transcendentals=0),
    )(owner_table, owner_table.reshape(1, NF), grad, left_factor, right_factor, left_root, right_root)
    shapes = tuple(jax.ShapeDtypeStruct(x.shape, x.dtype) for x in results)
    return pl.pallas_call(
        copy_out,
        out_shape=shapes,
        in_specs=[hbm] * 3,
        out_specs=(hbm,) * 3,
        scratch_shapes=[pltpu.SemaphoreType.DMA((3,))],
        compiler_params=pltpu.CompilerParams(vmem_limit_bytes=56 * 1024 * 1024),
    )(*results)


def solution(mesh):
    placed = (
        P(None, "fsdp", None),
        P("fsdp", "rep", None),
        P("fsdp", "rep", None),
        P("fsdp", "rep", None),
        P("fsdp", "rep", None),
        P(),
    )
    return jax.shard_map(
        body,
        mesh=mesh,
        in_specs=placed,
        out_specs=(P("fsdp", "rep", None), P("fsdp", "rep", None), P(None, "fsdp", "rep")),
        check_vma=False,
    )
```

```python
import jax
import jax.numpy as jnp
from jax import lax
from jax.experimental import pallas as pl
from jax.experimental.pallas import tpu as pltpu
from jax.sharding import PartitionSpec as P

moment_decay = 0.9
MESH = pl.DeviceIdType.MESH
bf16 = jnp.bfloat16
f32 = jnp.float32
i32 = jnp.int32

NF, NX = 128, 4
IN0, IN1, OUT, LA, LB, LFA, LFB = range(7)
XA0, XA1, XB0, XB1, XFA, XFB = range(6)


def split(x):
    hi = x.astype(bf16)
    return hi, (x - hi.astype(f32)).astype(bf16)


def dot3(a, b, dims):
    def one(p, q):
        return lax.dot_general(p, q, (dims, ((), ())), preferred_element_type=f32)

    return one(a[0], b[0]) + (one(a[0], b[1]) + one(a[1], b[0]))


def kernel(
    row_ref, grad_ref, lf_ref, rf_ref, lroot_ref, rroot_ref,
    left_out, right_out, dir_out,
    gq, send, gbuf, band, acc, ghi, glo, lown, lbuf, lhi, llo, rr, rhi, rlo, lf, rf, dbuf, rbuf,
    left_new, right_new, dir_new, row_v, tab_v, tab_s,
    send_sem, recv_sem, x_send_sem, x_recv_sem, loc_sem, in_sem, out_sem,
):
    me, r = lax.axis_index("fsdp"), lax.axis_index("rep")
    chip, core = lax.div(me, 2), lax.rem(me, 2)
    xa, xb, xc = lax.rem(r + 1, NX), lax.rem(r + 3, NX), lax.rem(r + 2, NX)

    def at128(q):
        return pl.ds(pl.multiple_of(q * 128, 128), 128)

    def load(src, dst, i):
        c = pltpu.make_async_copy(src, dst, in_sem.at[i])
        c.start()
        return c

    in_o = load(row_ref, row_v, 5)
    in_g = load(grad_ref.at[:, :, at128(r)], gq, 0)
    in_l = load(lroot_ref, lown, 1)
    in_r = load(rroot_ref, rr, 2)
    in_lf = load(lf_ref, lf, 3)
    in_rf = load(rf_ref, rf, 4)

    barrier = pltpu.get_barrier_semaphore()

    @pl.loop(0, NF // 8)
    def _(t):
        far = NF // 16 + lax.div(t + 1, 2) * (1 - 2 * lax.rem(t, 2))
        for i in range(8):
            f = lax.rem(me + far * 8 + i, NF)

            @pl.when(f != me)
            def _():
                pl.semaphore_signal(barrier, inc=1, device_id=(f, r), device_id_type=MESH)

    for x in (xa, xb):
        pl.semaphore_signal(barrier, inc=1, device_id=(me, x), device_id_type=MESH)

    in_o.wait()
    row = row_v[...]
    owner_of = jnp.transpose(jnp.broadcast_to(row, (NF, NF)))
    block = lax.broadcasted_iota(i32, (NF, NF), 0)
    lane = lax.broadcasted_iota(i32, (NF, NF), 1)
    match = owner_of == lane
    first = jnp.min(jnp.where(match, block, NF), axis=0, keepdims=True)
    last = jnp.max(jnp.where(match, block, -1), axis=0, keepdims=True)
    tab_v[0:1, :] = jnp.minimum(first, NF - 1)
    tab_v[1:2, :] = jnp.maximum(last, 0)
    later = jnp.max(jnp.where((owner_of == row) & (block < lane), 1, 0), axis=0, keepdims=True)
    tab_v[2:3, :] = later * NF + row
    to_s = pltpu.make_async_copy(tab_v, tab_s, loc_sem.at[2, 0])
    to_s.start()
    mine = lane[:1, :] == me
    live0 = jnp.max(jnp.where(mine & (first < NF), 1, 0), axis=1, keepdims=True)
    live1 = jnp.max(jnp.where(mine & (last > first), 1, 0), axis=1, keepdims=True)
    live = (live0, live1)

    def remote(src, dst, kind, k, dev):
        return pltpu.make_async_remote_copy(
            src_ref=src, dst_ref=dst, send_sem=send_sem.at[kind, k], recv_sem=recv_sem.at[kind, k],
            device_id=dev, device_id_type=MESH,
        )

    def wait_bytes(ref, sem):
        pltpu.make_async_copy(ref, ref, sem).wait()

    to_a, to_b = (me, xa), (me, xb)

    to_s.wait()
    in_g.wait()

    def pack(k):
        @pl.loop(0, NF, unroll=8)
        def _(o):
            send[k, o] = gq[tab_s[k, o]]

    pack(0)
    pl.semaphore_wait(barrier, NF - 1 + 2)

    def send_in(k, cc):
        @pl.when(core != cc)
        def _():
            o = chip * 2 + cc
            remote(send.at[k, o], gbuf.at[k, r, core], IN1, k, (o, r)).start()

        def piece(j, kind):
            o = lax.rem(chip + j, NF // 2) * 2 + cc
            remote(send.at[k, o], gbuf.at[k, r, (NF // 2 - j) * 2 + core], kind, k, (o, r)).start()

        @pl.loop(1, 33, unroll=4)
        def _(j):
            piece(j, IN0)

        @pl.loop(33, NF // 2)
        def _(j):
            piece(j, IN1)

    def own_copy(src, dst, i, k):
        c = pltpu.make_async_copy(src, dst, loc_sem.at[i, k])
        c.start()
        return c

    own_in = [None, None]
    send_in(0, 0)
    in_l.wait()

    def l_start(k):
        def block_to(q, slot, kind, dev):
            remote(lown.at[k, :, at128(q)], lbuf.at[k, slot], kind, k, dev).start()

        block_to(r, 0, LA, to_b)
        block_to(r, 3, LB, to_a)
        block_to(xa, 1, LA, to_b)
        block_to(xb, 4, LB, to_a)
        if k == 0:
            block_to(xc, 2, LA, to_b)
        else:
            block_to(xc, 2, LB, to_a)

    l_start(0)
    send_in(0, 1)
    own_in[0] = own_copy(send.at[0, me], gbuf.at[0, r, core], 0, 0)
    l_start(1)
    pack(1)
    send_in(1, 0)
    send_in(1, 1)
    own_in[1] = own_copy(send.at[1, me], gbuf.at[1, r, core], 0, 1)

    from_a = (pl.ds(0, 3), pl.ds(0, 2))
    from_b = (pl.ds(3, 2), pl.ds(2, 3))

    def l_forward(k):
        wait_bytes(lbuf.at[k, from_a[k]], recv_sem.at[LA, k])
        remote(lbuf.at[k, 0, pl.ds(0, 64)], lbuf.at[k, 5, pl.ds(0, 64)], LFA, k, to_b).start()
        wait_bytes(lbuf.at[k, from_b[k]], recv_sem.at[LB, k])
        remote(lbuf.at[k, 3, pl.ds(64, 64)], lbuf.at[k, 5, pl.ds(64, 64)], LFB, k, to_a).start()

    def l_put(k, p, q, x):
        hi, lo = split(x)
        lhi[k, at128(p), at128(q)] = hi
        llo[k, at128(p), at128(q)] = lo

    def l_both(k, p, q, x):
        l_put(k, p, q, x)
        l_put(k, q, p, jnp.transpose(x))

    def l_own(k):
        l_put(k, r, r, lown[k, :, at128(r)])
        for q in (xa, xb, xc):
            l_both(k, r, q, lown[k, :, at128(q)])

    def l_take(k):
        l_put(k, xa, xa, lbuf[k, 0])
        l_both(k, xa, xc, lbuf[k, 1])
        if k == 0:
            l_both(k, xa, xb, lbuf[k, 2])
        else:
            l_both(k, xb, xa, lbuf[k, 2])
        l_put(k, xb, xb, lbuf[k, 3])
        l_both(k, xb, xc, lbuf[k, 4])

    def l_end(k):
        wait_bytes(lbuf.at[k, 5, pl.ds(0, 64)], recv_sem.at[LFA, k])
        wait_bytes(lbuf.at[k, 5, pl.ds(64, 64)], recv_sem.at[LFB, k])
        l_put(k, xc, xc, lbuf[k, 5])

    half_at = (64, 0)

    def quarters(k, q, h):
        return gbuf.at[k, q, pl.ds(half_at[h], 32)], gbuf.at[k, q, pl.ds(half_at[h] + 32, 32)]

    def x_remote(ref, kind, k, h, dev):
        pltpu.make_async_remote_copy(
            src_ref=ref, dst_ref=ref, send_sem=x_send_sem.at[kind, k, h], recv_sem=x_recv_sem.at[kind, k, h],
            device_id=dev, device_id_type=MESH,
        ).start()

    def x_start(k, h):
        if h == 0:
            wait_bytes(gbuf.at[k, r, pl.ds(64, 64)], recv_sem.at[IN0, k])
        else:
            wait_bytes(gbuf.at[k, r, pl.ds(0, 63)], recv_sem.at[IN1, k])
            own_in[k].wait()
        g0, g1 = quarters(k, r, h)
        x_remote(g0, XA0, k, h, to_a)
        x_remote(g1, XB1, k, h, to_b)
        x_remote(g1, XA1, k, h, to_a)
        x_remote(g0, XB0, k, h, to_b)

    def x_forward(k, h):
        g0, _ = quarters(k, xb, h)
        wait_bytes(g0, x_recv_sem.at[XA0, k, h])
        x_remote(g0, XFA, k, h, to_a)
        _, g1 = quarters(k, xa, h)
        wait_bytes(g1, x_recv_sem.at[XB1, k, h])
        x_remote(g1, XFB, k, h, to_b)

    def take(k, q, start=False):
        @pl.loop(0, 8)
        def _(i):
            for j in range(8):
                m = i * 8 + j
                base = pl.multiple_of(lax.rem(chip + m, NF // 2) * 8, 8)
                band[pl.ds(base, 4), :] = gbuf[k, q, 2 * m]
                band[pl.ds(base + 4, 4), :] = gbuf[k, q, 2 * m + 1]

        g = split(band[...])
        ghi[k, :, at128(q)], glo[k, :, at128(q)] = g
        part = dot3(g, (rhi[k, at128(q), :], rlo[k, at128(q), :]), ((1,), (0,)))
        if start:
            acc[...] = part
        else:
            acc[...] += part

    def x_take_near(k):
        for h in range(2):
            _, g1 = quarters(k, xb, h)
            wait_bytes(g1, x_recv_sem.at[XA1, k, h])
        take(k, xb)
        for h in range(2):
            g0, _ = quarters(k, xa, h)
            wait_bytes(g0, x_recv_sem.at[XB0, k, h])
        take(k, xa)

    def x_take_far(k):
        for h in range(2):
            g0, g1 = quarters(k, xc, h)
            wait_bytes(g0, x_recv_sem.at[XFA, k, h])
            wait_bytes(g1, x_recv_sem.at[XFB, k, h])
        take(k, xc)

    def steer_and_send(k):
        t = split(acc[...])

        @pl.loop(0, 4)
        def _(i):
            p = lax.rem(lax.div(chip, 16) + i, 4)
            band[pl.ds(0, 128), :] = dot3((lhi[k, at128(p), :], llo[k, at128(p), :]), t, ((1,), (0,)))
            for j in range(32):
                dbuf[k, p * 32 + j] = band[pl.ds(j * 4, 4), :]

            def piece(j):
                f = p * 32 + lax.rem(me + j, 32)
                remote(dbuf.at[k, f], rbuf.at[k * NF + me], OUT, k, (f, r)).start()

            @pl.when(i > 0)
            def _():
                piece(0)

            pl.loop(1, 32)(piece)

        return own_copy(dbuf.at[k, me], rbuf.at[k * NF + me], 1, k)

    weight = (1.0 - moment_decay) / 512

    def stats(k):
        g = (ghi[k], glo[k])
        term = dot3((ghi[k, at128(r), :], glo[k, at128(r), :]), g, ((1,), (1,)))
        old = lf[k]
        left_new[k] = jnp.where(live[k] > 0, moment_decay * old + weight * term, old)
        term = dot3((ghi[k, :, at128(r)], glo[k, :, at128(r)]), g, ((0,), (0,)))
        old = rf[k]
        right_new[k] = jnp.where(live[k] > 0, moment_decay * old + weight * term, old)

    l_own(0)
    l_own(1)
    in_r.wait()
    for k in range(2):
        rhi[k], rlo[k] = split(jnp.transpose(rr[k]))
    l_forward(0)
    l_take(0)
    x_start(0, 0)
    x_start(0, 1)
    take(0, r, True)
    x_forward(0, 0)
    l_forward(1)
    x_forward(0, 1)
    l_end(0)
    x_take_near(0)
    x_start(1, 0)
    x_take_far(0)
    own_out0 = steer_and_send(0)
    x_start(1, 1)
    x_forward(1, 0)
    take(1, r, True)
    x_forward(1, 1)
    l_take(1)
    l_end(1)
    x_take_near(1)
    x_take_far(1)
    own_out1 = steer_and_send(1)
    in_lf.wait()
    in_rf.wait()
    stats(0)
    stats(1)
    out_l = pltpu.make_async_copy(left_new, left_out, out_sem.at[0])
    out_l.start()
    out_r = pltpu.make_async_copy(right_new, right_out, out_sem.at[1])
    out_r.start()

    own_outs = (own_out0, own_out1)
    for k in range(2):
        wait_bytes(rbuf.at[pl.ds(k * NF, NF - 1)], recv_sem.at[OUT, k])
        own_outs[k].wait()

    @pl.loop(0, NF, unroll=8)
    def _(b):
        dir_new[b] = rbuf[tab_s[2, b]]

    out_d = pltpu.make_async_copy(dir_new, dir_out, out_sem.at[2])
    out_d.start()
    for k in range(2):
        wait_bytes(gbuf.at[k, r, pl.ds(64, 64)], send_sem.at[IN0, k])
        wait_bytes(gbuf.at[k, r, pl.ds(0, 63)], send_sem.at[IN1, k])
        wait_bytes(rbuf.at[pl.ds(k * NF, NF - 1)], send_sem.at[OUT, k])
        for kind in (XA0, XA1, XB0, XB1, XFA, XFB):
            for h in range(2):
                wait_bytes(gbuf.at[k, r, pl.ds(0, 32)], x_send_sem.at[kind, k, h])
        wait_bytes(lbuf.at[k, from_a[k]], send_sem.at[LA, k])
        wait_bytes(lbuf.at[k, from_b[k]], send_sem.at[LB, k])
        for kind in (LFA, LFB):
            wait_bytes(lbuf.at[k, 5, pl.ds(0, 64)], send_sem.at[kind, k])
    out_l.wait()
    out_r.wait()
    out_d.wait()


def copy_out(a, b, c, a_out, b_out, c_out, sem):
    copies = [
        pltpu.make_async_copy(src, dst, sem.at[i])
        for i, (src, dst) in enumerate(((a, a_out), (b, b_out), (c, c_out)))
    ]
    for c in copies:
        c.start()
    for c in copies:
        c.wait()


def body(grad, left_factor, right_factor, left_root, right_root, owner_table):
    hbm = pl.BlockSpec(memory_space=pltpu.HBM)
    pieces = (2, NF, 4, 128)
    results = pl.pallas_call(
        kernel,
        out_shape=(
            jax.ShapeDtypeStruct((2, 128, 512), f32),
            jax.ShapeDtypeStruct((2, 128, 512), f32),
            jax.ShapeDtypeStruct((NF, 4, 128), f32),
        ),
        in_specs=[hbm] * 6,
        out_specs=(hbm, hbm, hbm),
        scratch_shapes=[
            pltpu.VMEM((NF, 4, 128), f32),
            pltpu.VMEM(pieces, f32),
            pltpu.VMEM((2, NX, NF, 4, 128), f32),
            pltpu.VMEM((512, 128), f32),
            pltpu.VMEM((512, 128), f32),
            pltpu.VMEM((2, 512, 512), bf16),
            pltpu.VMEM((2, 512, 512), bf16),
            pltpu.VMEM((2, 128, 512), f32),
            pltpu.VMEM((2, 6, 128, 128), f32),
            pltpu.VMEM((2, 512, 512), bf16),
            pltpu.VMEM((2, 512, 512), bf16),
            pltpu.VMEM((2, 128, 512), f32),
            pltpu.VMEM((2, 512, 128), bf16),
            pltpu.VMEM((2, 512, 128), bf16),
            pltpu.VMEM((2, 128, 512), f32),
            pltpu.VMEM((2, 128, 512), f32),
            pltpu.VMEM(pieces, f32),
            pltpu.VMEM((2 * NF, 4, 128), f32),
            pltpu.VMEM((2, 128, 512), f32),
            pltpu.VMEM((2, 128, 512), f32),
            pltpu.VMEM((NF, 4, 128), f32),
            pltpu.VMEM((1, 128), i32),
            pltpu.VMEM((8, 128), i32),
            pltpu.SMEM((8, 128), i32),
            pltpu.SemaphoreType.DMA((7, 2)),
            pltpu.SemaphoreType.DMA((7, 2)),
            pltpu.SemaphoreType.DMA((6, 2, 2)),
            pltpu.SemaphoreType.DMA((6, 2, 2)),
            pltpu.SemaphoreType.DMA((3, 2)),
            pltpu.SemaphoreType.DMA((6,)),
            pltpu.SemaphoreType.DMA((3,)),
        ],
        compiler_params=pltpu.CompilerParams(
            collective_id=0, has_side_effects=True, vmem_limit_bytes=55050240
        ),
        cost_estimate=pl.CostEstimate(flops=1610612736, bytes_accessed=4500000, transcendentals=0),
    )(owner_table.reshape(1, NF), grad, left_factor, right_factor, left_root, right_root)
    shapes = tuple(jax.ShapeDtypeStruct(x.shape, x.dtype) for x in results)
    return pl.pallas_call(
        copy_out,
        out_shape=shapes,
        in_specs=[hbm] * 3,
        out_specs=(hbm,) * 3,
        scratch_shapes=[pltpu.SemaphoreType.DMA((3,))],
        compiler_params=pltpu.CompilerParams(vmem_limit_bytes=4 * 1024 * 1024),
    )(*results)


def solution(mesh):
    placed = (
        P(None, "fsdp", None),
        P("fsdp", "rep", None),
        P("fsdp", "rep", None),
        P("fsdp", "rep", None),
        P("fsdp", "rep", None),
        P(),
    )
    return jax.shard_map(
        body,
        mesh=mesh,
        in_specs=placed,
        out_specs=(P("fsdp", "rep", None), P("fsdp", "rep", None), P(None, "fsdp", "rep")),
        check_vma=False,
    )
```

```python
import jax
import jax.numpy as jnp
from jax import lax
from jax.experimental import pallas as pl
from jax.experimental.pallas import tpu as pltpu
from jax.sharding import PartitionSpec as P

moment_decay = 0.9
MESH = pl.DeviceIdType.MESH
bf16 = jnp.bfloat16
f32 = jnp.float32
i32 = jnp.int32

NF, NX = 128, 4
OUT, LA, LB, LC = range(4)
XA, XB, XC = range(3)
NQ = 4


def split(x):
    hi = x.astype(bf16)
    return hi, (x - hi.astype(f32)).astype(bf16)


def dot3(a, b, dims):
    def one(p, q):
        return lax.dot_general(p, q, (dims, ((), ())), preferred_element_type=f32)

    return one(a[0], b[0]) + (one(a[0], b[1]) + one(a[1], b[0]))


def kernel(
    row_ref, grad_ref, lf_ref, rf_ref, lroot_ref, rroot_ref,
    left_out, right_out, dir_out,
    gq, send, gbuf, band, acc, ghi, glo, lown, lbuf, lhi, llo, rr, rhi, rlo, lf, rf, dbuf, rbuf,
    left_new, right_new, dir_new, row_v, tab_v, tab_s,
    send_sem, recv_sem, p_send_sem, p_recv_sem, x_send_sem, x_recv_sem, loc_sem, in_sem, out_sem,
):
    me, r = lax.axis_index("fsdp"), lax.axis_index("rep")
    chip, core = lax.div(me, 2), lax.rem(me, 2)
    xa, xb, xc = lax.rem(r + 1, NX), lax.rem(r + 3, NX), lax.rem(r + 2, NX)

    def at128(q):
        return pl.ds(pl.multiple_of(q * 128, 128), 128)

    def load(src, dst, i):
        c = pltpu.make_async_copy(src, dst, in_sem.at[i])
        c.start()
        return c

    in_o = load(row_ref, row_v, 5)
    in_g = load(grad_ref.at[:, :, at128(r)], gq, 0)
    in_l = load(lroot_ref, lown, 1)
    in_r = load(rroot_ref, rr, 2)
    in_lf = load(lf_ref, lf, 3)
    in_rf = load(rf_ref, rf, 4)

    barrier = pltpu.get_barrier_semaphore()

    @pl.loop(0, NF // 8)
    def _(t):
        far = NF // 16 + lax.div(t + 1, 2) * (1 - 2 * lax.rem(t, 2))
        for i in range(8):
            f = lax.rem(me + far * 8 + i, NF)

            @pl.when(f != me)
            def _():
                pl.semaphore_signal(barrier, inc=1, device_id=(f, r), device_id_type=MESH)

    for x in (xa, xb, xc):
        pl.semaphore_signal(barrier, inc=1, device_id=(me, x), device_id_type=MESH)

    in_o.wait()
    row = row_v[...]
    owner_of = jnp.transpose(jnp.broadcast_to(row, (NF, NF)))
    block = lax.broadcasted_iota(i32, (NF, NF), 0)
    lane = lax.broadcasted_iota(i32, (NF, NF), 1)
    match = owner_of == lane
    first = jnp.min(jnp.where(match, block, NF), axis=0, keepdims=True)
    last = jnp.max(jnp.where(match, block, -1), axis=0, keepdims=True)
    tab_v[0:1, :] = jnp.minimum(first, NF - 1)
    tab_v[1:2, :] = jnp.maximum(last, 0)
    later = jnp.max(jnp.where((owner_of == row) & (block < lane), 1, 0), axis=0, keepdims=True)
    tab_v[2:3, :] = later * NF + row
    to_s = pltpu.make_async_copy(tab_v, tab_s, loc_sem.at[2, 0])
    to_s.start()
    mine = lane[:1, :] == me
    live0 = jnp.max(jnp.where(mine & (first < NF), 1, 0), axis=1, keepdims=True)
    live1 = jnp.max(jnp.where(mine & (last > first), 1, 0), axis=1, keepdims=True)
    live = (live0, live1)

    def remote(src, dst, kind, k, dev):
        return pltpu.make_async_remote_copy(
            src_ref=src, dst_ref=dst, send_sem=send_sem.at[kind, k], recv_sem=recv_sem.at[kind, k],
            device_id=dev, device_id_type=MESH,
        )

    def wait_bytes(ref, sem):
        pltpu.make_async_copy(ref, ref, sem).wait()

    to_a, to_b, to_c = (me, xa), (me, xb), (me, xc)

    to_s.wait()
    in_g.wait()

    def pack(k):
        @pl.loop(0, NF, unroll=8)
        def _(o):
            send[k, o] = gq[tab_s[k, o]]

    pack(0)
    pl.semaphore_wait(barrier, NF - 1 + 3)

    def send_in(k, cc):
        def piece(o, place, h):
            pltpu.make_async_remote_copy(
                src_ref=send.at[k, o], dst_ref=gbuf.at[k, r, place],
                send_sem=p_send_sem.at[k, h], recv_sem=p_recv_sem.at[k, h],
                device_id=(o, r), device_id_type=MESH,
            ).start()

        @pl.when(core != cc)
        def _():
            piece(chip * 2 + cc, core, NQ - 1)

        @pl.loop(1, NF // 2)
        def _(j):
            o = lax.rem(chip + j, NF // 2) * 2 + cc
            piece(o, (NF // 2 - j) * 2 + core, lax.div(j - 1, 16))

    def own_copy(src, dst, i, k):
        c = pltpu.make_async_copy(src, dst, loc_sem.at[i, k])
        c.start()
        return c

    own_in = [None, None]
    send_in(0, 0)
    in_l.wait()

    def l_start(k):
        def block_to(q, slot, kind, dev):
            remote(lown.at[k, :, at128(q)], lbuf.at[k, slot], kind, k, dev).start()

        block_to(r, 0, LA, to_b)
        block_to(r, 3, LB, to_a)
        block_to(xa, 1, LA, to_b)
        block_to(xb, 4, LB, to_a)
        if k == 0:
            block_to(xc, 2, LA, to_b)
        else:
            block_to(xc, 2, LB, to_a)
        block_to(r, 5, LC, to_c)

    l_start(0)
    send_in(0, 1)
    own_in[0] = own_copy(send.at[0, me], gbuf.at[0, r, core], 0, 0)
    l_start(1)
    pack(1)
    send_in(1, 0)
    send_in(1, 1)
    own_in[1] = own_copy(send.at[1, me], gbuf.at[1, r, core], 0, 1)

    from_a = (pl.ds(0, 3), pl.ds(0, 2))
    from_b = (pl.ds(3, 2), pl.ds(2, 3))

    def l_put(k, p, q, x):
        hi, lo = split(x)
        lhi[k, at128(p), at128(q)] = hi
        llo[k, at128(p), at128(q)] = lo

    def l_both(k, p, q, x):
        l_put(k, p, q, x)
        l_put(k, q, p, jnp.transpose(x))

    def l_own(k):
        l_put(k, r, r, lown[k, :, at128(r)])
        for q in (xa, xb, xc):
            l_both(k, r, q, lown[k, :, at128(q)])

    def l_take(k):
        wait_bytes(lbuf.at[k, from_a[k]], recv_sem.at[LA, k])
        wait_bytes(lbuf.at[k, from_b[k]], recv_sem.at[LB, k])
        wait_bytes(lbuf.at[k, 5], recv_sem.at[LC, k])
        l_put(k, xc, xc, lbuf[k, 5])
        l_put(k, xa, xa, lbuf[k, 0])
        l_both(k, xa, xc, lbuf[k, 1])
        if k == 0:
            l_both(k, xa, xb, lbuf[k, 2])
        else:
            l_both(k, xb, xa, lbuf[k, 2])
        l_put(k, xb, xb, lbuf[k, 3])
        l_both(k, xb, xc, lbuf[k, 4])

    def quarter(k, q, h):
        return gbuf.at[k, q, pl.ds((NQ - 1 - h) * 32, 32)]

    def arrivals(k, h):
        return gbuf.at[k, r, pl.ds((NQ - 1 - h) * 32, 32 if h < NQ - 1 else 31)]

    def x_start(k, h):
        wait_bytes(arrivals(k, h), p_recv_sem.at[k, h])
        if h == NQ - 1:
            own_in[k].wait()
        g = quarter(k, r, h)
        for kind, dev in ((XC, to_c), (XA, to_a), (XB, to_b)):
            pltpu.make_async_remote_copy(
                src_ref=g, dst_ref=g, send_sem=x_send_sem.at[kind, k, h], recv_sem=x_recv_sem.at[kind, k, h],
                device_id=dev, device_id_type=MESH,
            ).start()

    def take(k, q, start=False):
        @pl.loop(0, 8)
        def _(i):
            for j in range(8):
                m = i * 8 + j
                base = pl.multiple_of(lax.rem(chip + m, NF // 2) * 8, 8)
                band[pl.ds(base, 4), :] = gbuf[k, q, 2 * m]
                band[pl.ds(base + 4, 4), :] = gbuf[k, q, 2 * m + 1]

        g = split(band[...])
        ghi[k, :, at128(q)], glo[k, :, at128(q)] = g
        part = dot3(g, (rhi[k, at128(q), :], rlo[k, at128(q), :]), ((1,), (0,)))
        if start:
            acc[...] = part
        else:
            acc[...] += part

    def x_take(k):
        for kind, q in ((XA, xb), (XB, xa), (XC, xc)):
            for h in range(NQ):
                wait_bytes(quarter(k, q, h), x_recv_sem.at[kind, k, h])
            take(k, q)

    def steer(k):
        return split(acc[...])

    def bands_out(k, t, start, stop):
        @pl.loop(start, stop)
        def _(i):
            p = lax.rem(lax.div(chip, 16) + i, 4)
            band[pl.ds(0, 128), :] = dot3((lhi[k, at128(p), :], llo[k, at128(p), :]), t, ((1,), (0,)))
            for j in range(32):
                dbuf[k, p * 32 + j] = band[pl.ds(j * 4, 4), :]

            def piece(j):
                f = p * 32 + lax.rem(me + j, 32)
                remote(dbuf.at[k, f], rbuf.at[k * NF + me], OUT, k, (f, r)).start()

            @pl.when(i > 0)
            def _():
                piece(0)

            pl.loop(1, 32)(piece)

    def own_piece_out(k):
        return own_copy(dbuf.at[k, me], rbuf.at[k * NF + me], 1, k)

    weight = (1.0 - moment_decay) / 512

    def stats(k):
        g = (ghi[k], glo[k])
        term = dot3((ghi[k, at128(r), :], glo[k, at128(r), :]), g, ((1,), (1,)))
        old = lf[k]
        left_new[k] = jnp.where(live[k] > 0, moment_decay * old + weight * term, old)
        term = dot3((ghi[k, :, at128(r)], glo[k, :, at128(r)]), g, ((0,), (0,)))
        old = rf[k]
        right_new[k] = jnp.where(live[k] > 0, moment_decay * old + weight * term, old)

    l_own(0)
    l_own(1)
    in_r.wait()
    for k in range(2):
        rhi[k], rlo[k] = split(jnp.transpose(rr[k]))
    for h in range(NQ - 1):
        x_start(0, h)
    l_take(0)
    x_start(0, NQ - 1)
    take(0, r, True)
    x_take(0)
    t = steer(0)
    bands_out(0, t, 0, 2)
    x_start(1, 0)
    bands_out(0, t, 2, 4)
    own_out0 = own_piece_out(0)
    x_start(1, 1)
    l_take(1)
    for h in range(2, NQ):
        x_start(1, h)
    take(1, r, True)
    x_take(1)
    t = steer(1)
    bands_out(1, t, 0, 4)
    own_out1 = own_piece_out(1)
    in_lf.wait()
    in_rf.wait()
    stats(0)
    stats(1)
    out_l = pltpu.make_async_copy(left_new, left_out, out_sem.at[0])
    out_l.start()
    out_r = pltpu.make_async_copy(right_new, right_out, out_sem.at[1])
    out_r.start()

    own_outs = (own_out0, own_out1)
    for k in range(2):
        wait_bytes(rbuf.at[pl.ds(k * NF, NF - 1)], recv_sem.at[OUT, k])
        own_outs[k].wait()

    @pl.loop(0, NF, unroll=8)
    def _(b):
        dir_new[b] = rbuf[tab_s[2, b]]

    out_d = pltpu.make_async_copy(dir_new, dir_out, out_sem.at[2])
    out_d.start()
    for k in range(2):
        for h in range(NQ):
            wait_bytes(arrivals(k, h), p_send_sem.at[k, h])
            for kind in (XA, XB, XC):
                wait_bytes(quarter(k, r, h), x_send_sem.at[kind, k, h])
        wait_bytes(rbuf.at[pl.ds(k * NF, NF - 1)], send_sem.at[OUT, k])
        wait_bytes(lbuf.at[k, from_a[k]], send_sem.at[LA, k])
        wait_bytes(lbuf.at[k, from_b[k]], send_sem.at[LB, k])
        wait_bytes(lbuf.at[k, 5], send_sem.at[LC, k])
    out_l.wait()
    out_r.wait()
    out_d.wait()


def copy_out(a, b, c, a_out, b_out, c_out, sem):
    copies = [
        pltpu.make_async_copy(src, dst, sem.at[i])
        for i, (src, dst) in enumerate(((a, a_out), (b, b_out), (c, c_out)))
    ]
    for c in copies:
        c.start()
    for c in copies:
        c.wait()


def body(grad, left_factor, right_factor, left_root, right_root, owner_table):
    hbm = pl.BlockSpec(memory_space=pltpu.HBM)
    pieces = (2, NF, 4, 128)
    results = pl.pallas_call(
        kernel,
        out_shape=(
            jax.ShapeDtypeStruct((2, 128, 512), f32),
            jax.ShapeDtypeStruct((2, 128, 512), f32),
            jax.ShapeDtypeStruct((NF, 4, 128), f32),
        ),
        in_specs=[hbm] * 6,
        out_specs=(hbm, hbm, hbm),
        scratch_shapes=[
            pltpu.VMEM((NF, 4, 128), f32),
            pltpu.VMEM(pieces, f32),
            pltpu.VMEM((2, NX, NF, 4, 128), f32),
            pltpu.VMEM((512, 128), f32),
            pltpu.VMEM((512, 128), f32),
            pltpu.VMEM((2, 512, 512), bf16),
            pltpu.VMEM((2, 512, 512), bf16),
            pltpu.VMEM((2, 128, 512), f32),
            pltpu.VMEM((2, 6, 128, 128), f32),
            pltpu.VMEM((2, 512, 512), bf16),
            pltpu.VMEM((2, 512, 512), bf16),
            pltpu.VMEM((2, 128, 512), f32),
            pltpu.VMEM((2, 512, 128), bf16),
            pltpu.VMEM((2, 512, 128), bf16),
            pltpu.VMEM((2, 128, 512), f32),
            pltpu.VMEM((2, 128, 512), f32),
            pltpu.VMEM(pieces, f32),
            pltpu.VMEM((2 * NF, 4, 128), f32),
            pltpu.VMEM((2, 128, 512), f32),
            pltpu.VMEM((2, 128, 512), f32),
            pltpu.VMEM((NF, 4, 128), f32),
            pltpu.VMEM((1, 128), i32),
            pltpu.VMEM((8, 128), i32),
            pltpu.SMEM((8, 128), i32),
            pltpu.SemaphoreType.DMA((4, 2)),
            pltpu.SemaphoreType.DMA((4, 2)),
            pltpu.SemaphoreType.DMA((2, NQ)),
            pltpu.SemaphoreType.DMA((2, NQ)),
            pltpu.SemaphoreType.DMA((3, 2, NQ)),
            pltpu.SemaphoreType.DMA((3, 2, NQ)),
            pltpu.SemaphoreType.DMA((3, 2)),
            pltpu.SemaphoreType.DMA((6,)),
            pltpu.SemaphoreType.DMA((3,)),
        ],
        compiler_params=pltpu.CompilerParams(
            collective_id=0, has_side_effects=True, vmem_limit_bytes=55050240
        ),
        cost_estimate=pl.CostEstimate(flops=1610612736, bytes_accessed=4500000, transcendentals=0),
    )(owner_table.reshape(1, NF), grad, left_factor, right_factor, left_root, right_root)
    shapes = tuple(jax.ShapeDtypeStruct(x.shape, x.dtype) for x in results)
    return pl.pallas_call(
        copy_out,
        out_shape=shapes,
        in_specs=[hbm] * 3,
        out_specs=(hbm,) * 3,
        scratch_shapes=[pltpu.SemaphoreType.DMA((3,))],
        compiler_params=pltpu.CompilerParams(vmem_limit_bytes=4 * 1024 * 1024),
    )(*results)


def solution(mesh):
    placed = (
        P(None, "fsdp", None),
        P("fsdp", "rep", None),
        P("fsdp", "rep", None),
        P("fsdp", "rep", None),
        P("fsdp", "rep", None),
        P(),
    )
    return jax.shard_map(
        body,
        mesh=mesh,
        in_specs=placed,
        out_specs=(P("fsdp", "rep", None), P("fsdp", "rep", None), P(None, "fsdp", "rep")),
        check_vma=False,
    )
```

```python
import jax
import jax.numpy as jnp
from jax import lax
from jax.experimental import pallas as pl
from jax.experimental.pallas import tpu as pltpu
from jax.sharding import PartitionSpec as P

moment_decay = 0.9
MESH = pl.DeviceIdType.MESH
bf16 = jnp.bfloat16
f32 = jnp.float32
i32 = jnp.int32

NF, NX = 128, 4
IN0, IN1, OUT, LA, LB, LFA, LFB = range(7)
XA0, XA1, XB0, XB1, XFA, XFB = range(6)


def split(x):
    hi = x.astype(bf16)
    return hi, (x - hi.astype(f32)).astype(bf16)


def dot3(a, b, dims):
    def one(p, q):
        return lax.dot_general(p, q, (dims, ((), ())), preferred_element_type=f32)

    return one(a[0], b[0]) + (one(a[0], b[1]) + one(a[1], b[0]))


def kernel(
    row_ref, grad_ref, lf_ref, rf_ref, lroot_ref, rroot_ref,
    left_out, right_out, dir_out,
    gq, send, gbuf, band, acc, ghi, glo, lown, lbuf, lhi, llo, rr, rhi, rlo, lf, rf, dbuf, rbuf,
    left_new, right_new, dir_new, row_v, tab_v, tab_s,
    send_sem, recv_sem, in_send_sem, x_send_sem, x_recv_sem, loc_sem, in_sem, out_sem,
):
    me, r = lax.axis_index("fsdp"), lax.axis_index("rep")
    chip, core = lax.div(me, 2), lax.rem(me, 2)
    xa, xb, xc = lax.rem(r + 1, NX), lax.rem(r + 3, NX), lax.rem(r + 2, NX)

    def far_first(i):
        return NF // 4 + lax.div(i + 1, 2) * (1 - 2 * lax.rem(i, 2))

    def at128(q):
        return pl.ds(pl.multiple_of(q * 128, 128), 128)

    def load(src, dst, i):
        c = pltpu.make_async_copy(src, dst, in_sem.at[i])
        c.start()
        return c

    in_o = load(row_ref, row_v, 5)
    in_g = load(grad_ref.at[:, :, at128(r)], gq, 0)
    in_l = load(lroot_ref, lown, 1)
    in_r = load(rroot_ref, rr, 2)
    in_lf = load(lf_ref, lf, 3)
    in_rf = load(rf_ref, rf, 4)

    barrier = pltpu.get_barrier_semaphore()

    @pl.loop(0, NF // 8)
    def _(t):
        far = NF // 16 + lax.div(t + 1, 2) * (1 - 2 * lax.rem(t, 2))
        for i in range(8):
            f = lax.rem(me + far * 8 + i, NF)

            @pl.when(f != me)
            def _():
                pl.semaphore_signal(barrier, inc=1, device_id=(f, r), device_id_type=MESH)

    for x in (xa, xb):
        pl.semaphore_signal(barrier, inc=1, device_id=(me, x), device_id_type=MESH)

    in_o.wait()
    row = row_v[...]
    owner_of = jnp.transpose(jnp.broadcast_to(row, (NF, NF)))
    block = lax.broadcasted_iota(i32, (NF, NF), 0)
    lane = lax.broadcasted_iota(i32, (NF, NF), 1)
    match = owner_of == lane
    first = jnp.min(jnp.where(match, block, NF), axis=0, keepdims=True)
    last = jnp.max(jnp.where(match, block, -1), axis=0, keepdims=True)
    tab_v[0:1, :] = jnp.minimum(first, NF - 1)
    tab_v[1:2, :] = jnp.maximum(last, 0)
    later = jnp.max(jnp.where((owner_of == row) & (block < lane), 1, 0), axis=0, keepdims=True)
    tab_v[2:3, :] = later * NF + row
    to_s = pltpu.make_async_copy(tab_v, tab_s, loc_sem.at[2, 0])
    to_s.start()
    mine = lane[:1, :] == me
    live0 = jnp.max(jnp.where(mine & (first < NF), 1, 0), axis=1, keepdims=True)
    live1 = jnp.max(jnp.where(mine & (last > first), 1, 0), axis=1, keepdims=True)
    live = (live0, live1)

    def remote(src, dst, kind, k, dev):
        return pltpu.make_async_remote_copy(
            src_ref=src, dst_ref=dst, send_sem=send_sem.at[kind, k], recv_sem=recv_sem.at[kind, k],
            device_id=dev, device_id_type=MESH,
        )

    def wait_bytes(ref, sem):
        pltpu.make_async_copy(ref, ref, sem).wait()

    to_a, to_b = (me, xa), (me, xb)

    to_s.wait()
    in_g.wait()

    def pack(k):
        @pl.loop(0, NF, unroll=8)
        def _(o):
            send[k, o] = gq[tab_s[k, o]]

    pack(0)
    pl.semaphore_wait(barrier, NF - 1 + 2)

    def send_in(k, cc):
        def piece(o, place, kind, sem):
            pltpu.make_async_remote_copy(
                src_ref=send.at[k, o], dst_ref=gbuf.at[k, r, place], send_sem=sem, recv_sem=recv_sem.at[kind, k],
                device_id=(o, r), device_id_type=MESH,
            ).start()

        @pl.when(core != cc)
        def _():
            piece(chip * 2 + cc, core, IN1, in_send_sem.at[k, 2, 0])

        def piece_to(i, kind, h):
            o = lax.rem(chip + far_first(i), NF // 2) * 2 + cc
            piece(o, (NF // 2 - 1 - i) * 2 + core, kind, in_send_sem.at[k, cc, h])

        @pl.loop(0, 32, unroll=4)
        def _(i):
            piece_to(i, IN0, 0)

        @pl.loop(32, NF // 2 - 1)
        def _(i):
            piece_to(i, IN1, 1)

    def in_sent(k, cc, h):
        wait_bytes(send.at[k, pl.ds(0, 32 - h)], in_send_sem.at[k, cc, h])

    def own_copy(src, dst, i, k):
        c = pltpu.make_async_copy(src, dst, loc_sem.at[i, k])
        c.start()
        return c

    own_in = [None, None]

    def l_start(k):
        def block_to(q, slot, kind, dev):
            remote(lown.at[k, :, at128(q)], lbuf.at[k, slot], kind, k, dev).start()

        block_to(r, 0, LA, to_b)
        block_to(r, 3, LB, to_a)
        block_to(xa, 1, LA, to_b)
        block_to(xb, 4, LB, to_a)
        if k == 0:
            block_to(xc, 2, LA, to_b)
        else:
            block_to(xc, 2, LB, to_a)

    from_a = (pl.ds(0, 3), pl.ds(0, 2))
    from_b = (pl.ds(3, 2), pl.ds(2, 3))

    def l_forward(k):
        wait_bytes(lbuf.at[k, from_a[k]], recv_sem.at[LA, k])
        remote(lbuf.at[k, 0, pl.ds(0, 64)], lbuf.at[k, 5, pl.ds(0, 64)], LFA, k, to_b).start()
        wait_bytes(lbuf.at[k, from_b[k]], recv_sem.at[LB, k])
        remote(lbuf.at[k, 3, pl.ds(64, 64)], lbuf.at[k, 5, pl.ds(64, 64)], LFB, k, to_a).start()

    def l_put(k, p, q, x):
        hi, lo = split(x)
        lhi[k, at128(p), at128(q)] = hi
        llo[k, at128(p), at128(q)] = lo

    def l_both(k, p, q, x):
        l_put(k, p, q, x)
        l_put(k, q, p, jnp.transpose(x))

    def l_own(k):
        l_put(k, r, r, lown[k, :, at128(r)])
        for q in (xa, xb, xc):
            l_both(k, r, q, lown[k, :, at128(q)])

    def l_take(k):
        l_put(k, xa, xa, lbuf[k, 0])
        l_both(k, xa, xc, lbuf[k, 1])
        if k == 0:
            l_both(k, xa, xb, lbuf[k, 2])
        else:
            l_both(k, xb, xa, lbuf[k, 2])
        l_put(k, xb, xb, lbuf[k, 3])
        l_both(k, xb, xc, lbuf[k, 4])

    def l_end(k):
        wait_bytes(lbuf.at[k, 5, pl.ds(0, 64)], recv_sem.at[LFA, k])
        wait_bytes(lbuf.at[k, 5, pl.ds(64, 64)], recv_sem.at[LFB, k])
        l_put(k, xc, xc, lbuf[k, 5])

    half_at = (64, 0)

    def quarters(k, q, h):
        return gbuf.at[k, q, pl.ds(half_at[h], 32)], gbuf.at[k, q, pl.ds(half_at[h] + 32, 32)]

    def x_remote(ref, kind, k, h, dev):
        pltpu.make_async_remote_copy(
            src_ref=ref, dst_ref=ref, send_sem=x_send_sem.at[kind, k, h], recv_sem=x_recv_sem.at[kind, k, h],
            device_id=dev, device_id_type=MESH,
        ).start()

    def x_start(k, h):
        if h == 0:
            wait_bytes(gbuf.at[k, r, pl.ds(64, 64)], recv_sem.at[IN0, k])
        else:
            wait_bytes(gbuf.at[k, r, pl.ds(0, 63)], recv_sem.at[IN1, k])
            own_in[k].wait()
        g0, g1 = quarters(k, r, h)
        x_remote(g0, XA0, k, h, to_a)
        x_remote(g1, XB1, k, h, to_b)
        x_remote(g1, XA1, k, h, to_a)
        x_remote(g0, XB0, k, h, to_b)

    def x_forward(k, h):
        g0, _ = quarters(k, xb, h)
        wait_bytes(g0, x_recv_sem.at[XA0, k, h])
        x_remote(g0, XFA, k, h, to_a)
        _, g1 = quarters(k, xa, h)
        wait_bytes(g1, x_recv_sem.at[XB1, k, h])
        x_remote(g1, XFB, k, h, to_b)

    def take(k, q, start=False):
        @pl.loop(0, 8)
        def _(i):
            for j in range(8):
                m = i * 8 + j
                source = lax.rem(chip + NF // 2 - far_first(NF // 2 - 1 - m), NF // 2)
                base = pl.multiple_of(source * 8, 8)
                band[pl.ds(base, 4), :] = gbuf[k, q, 2 * m]
                band[pl.ds(base + 4, 4), :] = gbuf[k, q, 2 * m + 1]

        g = split(band[...])
        ghi[k, :, at128(q)], glo[k, :, at128(q)] = g
        part = dot3(g, (rhi[k, at128(q), :], rlo[k, at128(q), :]), ((1,), (0,)))
        if start:
            acc[...] = part
        else:
            acc[...] += part

    def x_take_near(k):
        for h in range(2):
            _, g1 = quarters(k, xb, h)
            wait_bytes(g1, x_recv_sem.at[XA1, k, h])
        take(k, xb)
        for h in range(2):
            g0, _ = quarters(k, xa, h)
            wait_bytes(g0, x_recv_sem.at[XB0, k, h])
        take(k, xa)

    def x_take_far(k):
        for h in range(2):
            g0, g1 = quarters(k, xc, h)
            wait_bytes(g0, x_recv_sem.at[XFA, k, h])
            wait_bytes(g1, x_recv_sem.at[XFB, k, h])
        take(k, xc)

    def steer_and_send(k):
        t = split(acc[...])

        @pl.loop(0, 4)
        def _(p):
            band[at128(p), :] = dot3((lhi[k, at128(p), :], llo[k, at128(p), :]), t, ((1,), (0,)))

        @pl.loop(0, NF // 8)
        def _(i):
            for j in range(8):
                dbuf[k, i * 8 + j] = band[pl.ds(pl.multiple_of(i * 32, 32) + j * 4, 4), :]

        def piece(f):
            remote(dbuf.at[k, f], rbuf.at[k * NF + me], OUT, k, (f, r)).start()

        @pl.loop(0, NF // 2 - 1)
        def _(i):
            f = lax.rem(chip + far_first(i), NF // 2) * 2
            piece(f)
            piece(f + 1)

        piece(chip * 2 + 1 - core)

        return own_copy(dbuf.at[k, me], rbuf.at[k * NF + me], 1, k)

    weight = (1.0 - moment_decay) / 512

    def stats(k):
        g = (ghi[k], glo[k])
        term = dot3((ghi[k, at128(r), :], glo[k, at128(r), :]), g, ((1,), (1,)))
        old = lf[k]
        left_new[k] = jnp.where(live[k] > 0, moment_decay * old + weight * term, old)
        term = dot3((ghi[k, :, at128(r)], glo[k, :, at128(r)]), g, ((0,), (0,)))
        old = rf[k]
        right_new[k] = jnp.where(live[k] > 0, moment_decay * old + weight * term, old)

    send_in(0, 0)
    own_in[0] = own_copy(send.at[0, me], gbuf.at[0, r, core], 0, 0)
    in_l.wait()
    l_start(0)
    send_in(0, 1)
    pack(1)
    own_in[1] = own_copy(send.at[1, me], gbuf.at[1, r, core], 0, 1)
    send_in(1, 0)
    send_in(1, 1)
    l_own(0)
    l_own(1)
    in_r.wait()
    for k in range(2):
        rhi[k], rlo[k] = split(jnp.transpose(rr[k]))
    l_forward(0)
    l_take(0)
    x_start(0, 0)
    x_start(0, 1)
    take(0, r, True)
    x_forward(0, 0)
    x_forward(0, 1)
    l_start(1)
    l_end(0)
    x_take_near(0)
    x_take_far(0)
    own_out0 = steer_and_send(0)
    x_start(1, 0)
    x_start(1, 1)
    x_forward(1, 0)
    l_forward(1)
    take(1, r, True)
    x_forward(1, 1)
    l_take(1)
    l_end(1)
    x_take_near(1)
    x_take_far(1)
    own_out1 = steer_and_send(1)
    in_lf.wait()
    in_rf.wait()
    stats(0)
    stats(1)
    out_l = pltpu.make_async_copy(left_new, left_out, out_sem.at[0])
    out_l.start()
    out_r = pltpu.make_async_copy(right_new, right_out, out_sem.at[1])
    out_r.start()

    own_outs = (own_out0, own_out1)
    for k in range(2):
        wait_bytes(rbuf.at[pl.ds(k * NF, NF - 1)], recv_sem.at[OUT, k])
        own_outs[k].wait()

    @pl.loop(0, NF, unroll=8)
    def _(b):
        dir_new[b] = rbuf[tab_s[2, b]]

    out_d = pltpu.make_async_copy(dir_new, dir_out, out_sem.at[2])
    out_d.start()
    for k in range(2):
        wait_bytes(send.at[k, 0], in_send_sem.at[k, 2, 0])
        for cc in range(2):
            for h in range(2):
                in_sent(k, cc, h)
        wait_bytes(rbuf.at[pl.ds(k * NF, NF - 1)], send_sem.at[OUT, k])
        for kind in (XA0, XA1, XB0, XB1, XFA, XFB):
            for h in range(2):
                wait_bytes(gbuf.at[k, r, pl.ds(0, 32)], x_send_sem.at[kind, k, h])
        wait_bytes(lbuf.at[k, from_a[k]], send_sem.at[LA, k])
        wait_bytes(lbuf.at[k, from_b[k]], send_sem.at[LB, k])
        for kind in (LFA, LFB):
            wait_bytes(lbuf.at[k, 5, pl.ds(0, 64)], send_sem.at[kind, k])
    out_l.wait()
    out_r.wait()
    out_d.wait()


def copy_out(a, b, c, a_out, b_out, c_out, sem):
    copies = [
        pltpu.make_async_copy(src, dst, sem.at[i])
        for i, (src, dst) in enumerate(((a, a_out), (b, b_out), (c, c_out)))
    ]
    for c in copies:
        c.start()
    for c in copies:
        c.wait()


def body(grad, left_factor, right_factor, left_root, right_root, owner_table):
    hbm = pl.BlockSpec(memory_space=pltpu.HBM)
    pieces = (2, NF, 4, 128)
    results = pl.pallas_call(
        kernel,
        out_shape=(
            jax.ShapeDtypeStruct((2, 128, 512), f32),
            jax.ShapeDtypeStruct((2, 128, 512), f32),
            jax.ShapeDtypeStruct((NF, 4, 128), f32),
        ),
        in_specs=[hbm] * 6,
        out_specs=(hbm, hbm, hbm),
        scratch_shapes=[
            pltpu.VMEM((NF, 4, 128), f32),
            pltpu.VMEM(pieces, f32),
            pltpu.VMEM((2, NX, NF, 4, 128), f32),
            pltpu.VMEM((512, 128), f32),
            pltpu.VMEM((512, 128), f32),
            pltpu.VMEM((2, 512, 512), bf16),
            pltpu.VMEM((2, 512, 512), bf16),
            pltpu.VMEM((2, 128, 512), f32),
            pltpu.VMEM((2, 6, 128, 128), f32),
            pltpu.VMEM((2, 512, 512), bf16),
            pltpu.VMEM((2, 512, 512), bf16),
            pltpu.VMEM((2, 128, 512), f32),
            pltpu.VMEM((2, 512, 128), bf16),
            pltpu.VMEM((2, 512, 128), bf16),
            pltpu.VMEM((2, 128, 512), f32),
            pltpu.VMEM((2, 128, 512), f32),
            pltpu.VMEM(pieces, f32),
            pltpu.VMEM((2 * NF, 4, 128), f32),
            pltpu.VMEM((2, 128, 512), f32),
            pltpu.VMEM((2, 128, 512), f32),
            pltpu.VMEM((NF, 4, 128), f32),
            pltpu.VMEM((1, 128), i32),
            pltpu.VMEM((8, 128), i32),
            pltpu.SMEM((8, 128), i32),
            pltpu.SemaphoreType.DMA((7, 2)),
            pltpu.SemaphoreType.DMA((7, 2)),
            pltpu.SemaphoreType.DMA((2, 3, 2)),
            pltpu.SemaphoreType.DMA((6, 2, 2)),
            pltpu.SemaphoreType.DMA((6, 2, 2)),
            pltpu.SemaphoreType.DMA((3, 2)),
            pltpu.SemaphoreType.DMA((6,)),
            pltpu.SemaphoreType.DMA((3,)),
        ],
        compiler_params=pltpu.CompilerParams(
            collective_id=0, has_side_effects=True, vmem_limit_bytes=55050240
        ),
        cost_estimate=pl.CostEstimate(flops=1610612736, bytes_accessed=4500000, transcendentals=0),
    )(owner_table.reshape(1, NF), grad, left_factor, right_factor, left_root, right_root)
    shapes = tuple(jax.ShapeDtypeStruct(x.shape, x.dtype) for x in results)
    return pl.pallas_call(
        copy_out,
        out_shape=shapes,
        in_specs=[hbm] * 3,
        out_specs=(hbm,) * 3,
        scratch_shapes=[pltpu.SemaphoreType.DMA((3,))],
        compiler_params=pltpu.CompilerParams(vmem_limit_bytes=4 * 1024 * 1024),
    )(*results)


def solution(mesh):
    placed = (
        P(None, "fsdp", None),
        P("fsdp", "rep", None),
        P("fsdp", "rep", None),
        P("fsdp", "rep", None),
        P("fsdp", "rep", None),
        P(),
    )
    return jax.shard_map(
        body,
        mesh=mesh,
        in_specs=placed,
        out_specs=(P("fsdp", "rep", None), P("fsdp", "rep", None), P(None, "fsdp", "rep")),
        check_vma=False,
    )
```

```python
import jax
import jax.numpy as jnp
from jax import lax
from jax.experimental import pallas as pl
from jax.experimental.pallas import tpu as pltpu
from jax.sharding import PartitionSpec as P

moment_decay = 0.9
MESH = pl.DeviceIdType.MESH
bf16 = jnp.bfloat16
f32 = jnp.float32
i32 = jnp.int32

NF, NX = 128, 4
IN0, IN1, OUT, LA, LB, LFA, LFB = range(7)
XA0, XA1, XB0, XB1, XFA, XFB = range(6)


def split(x):
    hi = x.astype(bf16)
    return hi, (x - hi.astype(f32)).astype(bf16)


def dot3(a, b, dims):
    def one(p, q):
        return lax.dot_general(p, q, (dims, ((), ())), preferred_element_type=f32)

    return one(a[0], b[0]) + (one(a[0], b[1]) + one(a[1], b[0]))


def kernel(
    row_ref, grad_ref, lf_ref, rf_ref, lroot_ref, rroot_ref,
    left_out, right_out, dir_out,
    gq, send, gbuf, band, acc, ghi, glo, lown, lbuf, lhi, llo, rr, rhi, rlo, lf, rf, dbuf, rbuf,
    left_new, right_new, dir_new, row_v, tab_v, tab_s,
    send_sem, recv_sem, in_send_sem, x_send_sem, x_recv_sem, loc_sem, in_sem, out_sem,
):
    me, r = lax.axis_index("fsdp"), lax.axis_index("rep")
    chip, core = lax.div(me, 2), lax.rem(me, 2)
    xa, xb, xc = lax.rem(r + 1, NX), lax.rem(r + 3, NX), lax.rem(r + 2, NX)

    def far_first(i):
        return NF // 4 + lax.div(i + 1, 2) * (1 - 2 * lax.rem(i, 2))

    def at128(q):
        return pl.ds(pl.multiple_of(q * 128, 128), 128)

    def load(src, dst, i):
        c = pltpu.make_async_copy(src, dst, in_sem.at[i])
        c.start()
        return c

    in_o = load(row_ref, row_v, 5)
    in_g = load(grad_ref.at[:, :, at128(r)], gq, 0)
    in_l = load(lroot_ref, lown, 1)
    in_r = load(rroot_ref, rr, 2)
    in_lf = load(lf_ref, lf, 3)
    in_rf = load(rf_ref, rf, 4)

    barrier = pltpu.get_barrier_semaphore()

    @pl.loop(0, NF // 8)
    def _(t):
        far = NF // 16 + lax.div(t + 1, 2) * (1 - 2 * lax.rem(t, 2))
        for i in range(8):
            f = lax.rem(me + far * 8 + i, NF)

            @pl.when(f != me)
            def _():
                pl.semaphore_signal(barrier, inc=1, device_id=(f, r), device_id_type=MESH)

    for x in (xa, xb):
        pl.semaphore_signal(barrier, inc=1, device_id=(me, x), device_id_type=MESH)

    in_o.wait()
    row = row_v[...]
    owner_of = jnp.transpose(jnp.broadcast_to(row, (NF, NF)))
    block = lax.broadcasted_iota(i32, (NF, NF), 0)
    lane = lax.broadcasted_iota(i32, (NF, NF), 1)
    match = owner_of == lane
    first = jnp.min(jnp.where(match, block, NF), axis=0, keepdims=True)
    last = jnp.max(jnp.where(match, block, -1), axis=0, keepdims=True)
    tab_v[0:1, :] = jnp.minimum(first, NF - 1)
    tab_v[1:2, :] = jnp.maximum(last, 0)
    later = jnp.max(jnp.where((owner_of == row) & (block < lane), 1, 0), axis=0, keepdims=True)
    tab_v[2:3, :] = later * NF + row
    to_s = pltpu.make_async_copy(tab_v, tab_s, loc_sem.at[2, 0])
    to_s.start()
    mine = lane[:1, :] == me
    live0 = jnp.max(jnp.where(mine & (first < NF), 1, 0), axis=1, keepdims=True)
    live1 = jnp.max(jnp.where(mine & (last > first), 1, 0), axis=1, keepdims=True)
    live = (live0, live1)

    def remote(src, dst, kind, k, dev):
        return pltpu.make_async_remote_copy(
            src_ref=src, dst_ref=dst, send_sem=send_sem.at[kind, k], recv_sem=recv_sem.at[kind, k],
            device_id=dev, device_id_type=MESH,
        )

    def wait_bytes(ref, sem):
        pltpu.make_async_copy(ref, ref, sem).wait()

    to_a, to_b = (me, xa), (me, xb)

    to_s.wait()
    in_g.wait()

    def pack(k):
        @pl.loop(0, NF, unroll=8)
        def _(o):
            send[k, o] = gq[tab_s[k, o]]

    pack(0)
    pl.semaphore_wait(barrier, NF - 1 + 2)

    def send_in(k, cc):
        def piece(o, place, kind, sem):
            pltpu.make_async_remote_copy(
                src_ref=send.at[k, o], dst_ref=gbuf.at[k, r, place], send_sem=sem, recv_sem=recv_sem.at[kind, k],
                device_id=(o, r), device_id_type=MESH,
            ).start()

        @pl.when(core != cc)
        def _():
            piece(chip * 2 + cc, core, IN1, in_send_sem.at[k, 2, 0])

        def piece_to(i, kind, h):
            o = lax.rem(chip + far_first(i), NF // 2) * 2 + cc
            piece(o, (NF // 2 - 1 - i) * 2 + core, kind, in_send_sem.at[k, cc, h])

        @pl.loop(0, 32, unroll=4)
        def _(i):
            piece_to(i, IN0, 0)

        @pl.loop(32, NF // 2 - 1)
        def _(i):
            piece_to(i, IN1, 1)

    def in_sent(k, cc, h):
        wait_bytes(send.at[k, pl.ds(0, 32 - h)], in_send_sem.at[k, cc, h])

    def own_copy(src, dst, i, k):
        c = pltpu.make_async_copy(src, dst, loc_sem.at[i, k])
        c.start()
        return c

    own_in = [None, None]

    def l_start(k):
        def block_to(q, slot, kind, dev):
            remote(lown.at[k, :, at128(q)], lbuf.at[k, slot], kind, k, dev).start()

        block_to(r, 0, LA, to_b)
        block_to(r, 3, LB, to_a)
        block_to(xa, 1, LA, to_b)
        block_to(xb, 4, LB, to_a)
        if k == 0:
            block_to(xc, 2, LA, to_b)
        else:
            block_to(xc, 2, LB, to_a)

    from_a = (pl.ds(0, 3), pl.ds(0, 2))
    from_b = (pl.ds(3, 2), pl.ds(2, 3))

    def l_forward(k):
        wait_bytes(lbuf.at[k, from_a[k]], recv_sem.at[LA, k])
        remote(lbuf.at[k, 0, pl.ds(0, 64)], lbuf.at[k, 5, pl.ds(0, 64)], LFA, k, to_b).start()
        wait_bytes(lbuf.at[k, from_b[k]], recv_sem.at[LB, k])
        remote(lbuf.at[k, 3, pl.ds(64, 64)], lbuf.at[k, 5, pl.ds(64, 64)], LFB, k, to_a).start()

    def l_put(k, p, q, x):
        hi, lo = split(x)
        lhi[k, at128(p), at128(q)] = hi
        llo[k, at128(p), at128(q)] = lo

    def l_both(k, p, q, x):
        l_put(k, p, q, x)
        l_put(k, q, p, jnp.transpose(x))

    def l_own(k):
        l_put(k, r, r, lown[k, :, at128(r)])
        for q in (xa, xb, xc):
            l_both(k, r, q, lown[k, :, at128(q)])

    def l_take(k):
        l_put(k, xa, xa, lbuf[k, 0])
        l_both(k, xa, xc, lbuf[k, 1])
        if k == 0:
            l_both(k, xa, xb, lbuf[k, 2])
        else:
            l_both(k, xb, xa, lbuf[k, 2])
        l_put(k, xb, xb, lbuf[k, 3])
        l_both(k, xb, xc, lbuf[k, 4])

    def l_end(k):
        wait_bytes(lbuf.at[k, 5, pl.ds(0, 64)], recv_sem.at[LFA, k])
        wait_bytes(lbuf.at[k, 5, pl.ds(64, 64)], recv_sem.at[LFB, k])
        l_put(k, xc, xc, lbuf[k, 5])

    half_at = (64, 0)

    def quarters(k, q, h):
        return gbuf.at[k, q, pl.ds(half_at[h], 32)], gbuf.at[k, q, pl.ds(half_at[h] + 32, 32)]

    def x_remote(ref, kind, k, h, dev):
        pltpu.make_async_remote_copy(
            src_ref=ref, dst_ref=ref, send_sem=x_send_sem.at[kind, k, h], recv_sem=x_recv_sem.at[kind, k, h],
            device_id=dev, device_id_type=MESH,
        ).start()

    def x_start(k, h):
        if h == 0:
            wait_bytes(gbuf.at[k, r, pl.ds(64, 64)], recv_sem.at[IN0, k])
        else:
            wait_bytes(gbuf.at[k, r, pl.ds(0, 63)], recv_sem.at[IN1, k])
            own_in[k].wait()
        g0, g1 = quarters(k, r, h)
        x_remote(g0, XA0, k, h, to_a)
        x_remote(g1, XB1, k, h, to_b)
        x_remote(g1, XA1, k, h, to_a)
        x_remote(g0, XB0, k, h, to_b)

    def x_forward(k, h):
        g0, _ = quarters(k, xb, h)
        wait_bytes(g0, x_recv_sem.at[XA0, k, h])
        x_remote(g0, XFA, k, h, to_a)
        _, g1 = quarters(k, xa, h)
        wait_bytes(g1, x_recv_sem.at[XB1, k, h])
        x_remote(g1, XFB, k, h, to_b)

    def take(k, q, start=False):
        @pl.loop(0, 8)
        def _(i):
            for j in range(4):
                n = i * 4 + j
                for m, source in ((2 * n, chip + NF // 2 - n), (2 * n + 1, chip + 1 + n)):
                    base = pl.multiple_of(lax.rem(source, NF // 2) * 8, 8)
                    band[pl.ds(base, 4), :] = gbuf[k, q, 2 * m]
                    band[pl.ds(base + 4, 4), :] = gbuf[k, q, 2 * m + 1]

        g = split(band[...])
        ghi[k, :, at128(q)], glo[k, :, at128(q)] = g
        part = dot3(g, (rhi[k, at128(q), :], rlo[k, at128(q), :]), ((1,), (0,)))
        if start:
            acc[...] = part
        else:
            acc[...] += part

    def x_take_near(k):
        for h in range(2):
            _, g1 = quarters(k, xb, h)
            wait_bytes(g1, x_recv_sem.at[XA1, k, h])
        take(k, xb)
        for h in range(2):
            g0, _ = quarters(k, xa, h)
            wait_bytes(g0, x_recv_sem.at[XB0, k, h])
        take(k, xa)

    def x_take_far(k):
        for h in range(2):
            g0, g1 = quarters(k, xc, h)
            wait_bytes(g0, x_recv_sem.at[XFA, k, h])
            wait_bytes(g1, x_recv_sem.at[XFB, k, h])
        take(k, xc)

    def steer_and_send(k):
        t = split(acc[...])

        @pl.loop(0, 4)
        def _(p):
            band[at128(p), :] = dot3((lhi[k, at128(p), :], llo[k, at128(p), :]), t, ((1,), (0,)))

        @pl.loop(0, NF // 8)
        def _(i):
            for j in range(8):
                dbuf[k, i * 8 + j] = band[pl.ds(pl.multiple_of(i * 32, 32) + j * 4, 4), :]

        def piece(f):
            remote(dbuf.at[k, f], rbuf.at[k * NF + me], OUT, k, (f, r)).start()

        @pl.loop(0, NF // 2 - 1)
        def _(i):
            f = lax.rem(chip + far_first(i), NF // 2) * 2
            piece(f)
            piece(f + 1)

        piece(chip * 2 + 1 - core)

        return own_copy(dbuf.at[k, me], rbuf.at[k * NF + me], 1, k)

    weight = (1.0 - moment_decay) / 512

    def stats(k):
        g = (ghi[k], glo[k])
        term = dot3((ghi[k, at128(r), :], glo[k, at128(r), :]), g, ((1,), (1,)))
        old = lf[k]
        left_new[k] = jnp.where(live[k] > 0, moment_decay * old + weight * term, old)
        term = dot3((ghi[k, :, at128(r)], glo[k, :, at128(r)]), g, ((0,), (0,)))
        old = rf[k]
        right_new[k] = jnp.where(live[k] > 0, moment_decay * old + weight * term, old)

    send_in(0, 0)
    own_in[0] = own_copy(send.at[0, me], gbuf.at[0, r, core], 0, 0)
    in_l.wait()
    l_start(0)
    send_in(0, 1)
    pack(1)
    own_in[1] = own_copy(send.at[1, me], gbuf.at[1, r, core], 0, 1)
    send_in(1, 0)
    send_in(1, 1)
    l_own(0)
    l_own(1)
    in_r.wait()
    for k in range(2):
        rhi[k], rlo[k] = split(jnp.transpose(rr[k]))
    l_forward(0)
    l_take(0)
    x_start(0, 0)
    x_start(0, 1)
    take(0, r, True)
    x_forward(0, 0)
    x_forward(0, 1)
    l_start(1)
    l_end(0)
    x_take_near(0)
    x_take_far(0)
    own_out0 = steer_and_send(0)
    x_start(1, 0)
    x_start(1, 1)
    x_forward(1, 0)
    l_forward(1)
    take(1, r, True)
    x_forward(1, 1)
    l_take(1)
    l_end(1)
    x_take_near(1)
    x_take_far(1)
    own_out1 = steer_and_send(1)
    in_lf.wait()
    in_rf.wait()
    stats(0)
    stats(1)
    out_l = pltpu.make_async_copy(left_new, left_out, out_sem.at[0])
    out_l.start()
    out_r = pltpu.make_async_copy(right_new, right_out, out_sem.at[1])
    out_r.start()

    own_outs = (own_out0, own_out1)
    for k in range(2):
        wait_bytes(rbuf.at[pl.ds(k * NF, NF - 1)], recv_sem.at[OUT, k])
        own_outs[k].wait()

    @pl.loop(0, NF, unroll=8)
    def _(b):
        dir_new[b] = rbuf[tab_s[2, b]]

    out_d = pltpu.make_async_copy(dir_new, dir_out, out_sem.at[2])
    out_d.start()
    for k in range(2):
        wait_bytes(send.at[k, 0], in_send_sem.at[k, 2, 0])
        for cc in range(2):
            for h in range(2):
                in_sent(k, cc, h)
        wait_bytes(rbuf.at[pl.ds(k * NF, NF - 1)], send_sem.at[OUT, k])
        for kind in (XA0, XA1, XB0, XB1, XFA, XFB):
            for h in range(2):
                wait_bytes(gbuf.at[k, r, pl.ds(0, 32)], x_send_sem.at[kind, k, h])
        wait_bytes(lbuf.at[k, from_a[k]], send_sem.at[LA, k])
        wait_bytes(lbuf.at[k, from_b[k]], send_sem.at[LB, k])
        for kind in (LFA, LFB):
            wait_bytes(lbuf.at[k, 5, pl.ds(0, 64)], send_sem.at[kind, k])
    out_l.wait()
    out_r.wait()
    out_d.wait()


def copy_out(a, b, c, a_out, b_out, c_out, sem):
    copies = [
        pltpu.make_async_copy(src, dst, sem.at[i])
        for i, (src, dst) in enumerate(((a, a_out), (b, b_out), (c, c_out)))
    ]
    for c in copies:
        c.start()
    for c in copies:
        c.wait()


def body(grad, left_factor, right_factor, left_root, right_root, owner_table):
    hbm = pl.BlockSpec(memory_space=pltpu.HBM)
    pieces = (2, NF, 4, 128)
    results = pl.pallas_call(
        kernel,
        out_shape=(
            jax.ShapeDtypeStruct((2, 128, 512), f32),
            jax.ShapeDtypeStruct((2, 128, 512), f32),
            jax.ShapeDtypeStruct((NF, 4, 128), f32),
        ),
        in_specs=[hbm] * 6,
        out_specs=(hbm, hbm, hbm),
        scratch_shapes=[
            pltpu.VMEM((NF, 4, 128), f32),
            pltpu.VMEM(pieces, f32),
            pltpu.VMEM((2, NX, NF, 4, 128), f32),
            pltpu.VMEM((512, 128), f32),
            pltpu.VMEM((512, 128), f32),
            pltpu.VMEM((2, 512, 512), bf16),
            pltpu.VMEM((2, 512, 512), bf16),
            pltpu.VMEM((2, 128, 512), f32),
            pltpu.VMEM((2, 6, 128, 128), f32),
            pltpu.VMEM((2, 512, 512), bf16),
            pltpu.VMEM((2, 512, 512), bf16),
            pltpu.VMEM((2, 128, 512), f32),
            pltpu.VMEM((2, 512, 128), bf16),
            pltpu.VMEM((2, 512, 128), bf16),
            pltpu.VMEM((2, 128, 512), f32),
            pltpu.VMEM((2, 128, 512), f32),
            pltpu.VMEM(pieces, f32),
            pltpu.VMEM((2 * NF, 4, 128), f32),
            pltpu.VMEM((2, 128, 512), f32),
            pltpu.VMEM((2, 128, 512), f32),
            pltpu.VMEM((NF, 4, 128), f32),
            pltpu.VMEM((1, 128), i32),
            pltpu.VMEM((8, 128), i32),
            pltpu.SMEM((8, 128), i32),
            pltpu.SemaphoreType.DMA((7, 2)),
            pltpu.SemaphoreType.DMA((7, 2)),
            pltpu.SemaphoreType.DMA((2, 3, 2)),
            pltpu.SemaphoreType.DMA((6, 2, 2)),
            pltpu.SemaphoreType.DMA((6, 2, 2)),
            pltpu.SemaphoreType.DMA((3, 2)),
            pltpu.SemaphoreType.DMA((6,)),
            pltpu.SemaphoreType.DMA((3,)),
        ],
        compiler_params=pltpu.CompilerParams(
            collective_id=0, has_side_effects=True, vmem_limit_bytes=55050240
        ),
        cost_estimate=pl.CostEstimate(flops=1610612736, bytes_accessed=4500000, transcendentals=0),
    )(owner_table.reshape(1, NF), grad, left_factor, right_factor, left_root, right_root)
    shapes = tuple(jax.ShapeDtypeStruct(x.shape, x.dtype) for x in results)
    return pl.pallas_call(
        copy_out,
        out_shape=shapes,
        in_specs=[hbm] * 3,
        out_specs=(hbm,) * 3,
        scratch_shapes=[pltpu.SemaphoreType.DMA((3,))],
        compiler_params=pltpu.CompilerParams(vmem_limit_bytes=4 * 1024 * 1024),
    )(*results)


def solution(mesh):
    placed = (
        P(None, "fsdp", None),
        P("fsdp", "rep", None),
        P("fsdp", "rep", None),
        P("fsdp", "rep", None),
        P("fsdp", "rep", None),
        P(),
    )
    return jax.shard_map(
        body,
        mesh=mesh,
        in_specs=placed,
        out_specs=(P("fsdp", "rep", None), P("fsdp", "rep", None), P(None, "fsdp", "rep")),
        check_vma=False,
    )
```
